256 devices in a mesh: facet: 16 (over x, z_hi), freq: 16 (over z_lo, y, core).
Axes of the slice: x: 4, y: 4, z: 8 (z_hi: 4, z_lo: 2; z = z_hi * 2 + z_lo), core: 2. Of those that a mesh axis runs over, the one named last changes fastest.
Arguments:
- facet_image: bfloat16 [16, 2, 512, 4096], P('facet', None, 'freq'), may hold values from -6 to 6
- facet_offsets: int32 [16, 2], replicated, may hold values from 0 to 32767
- subgrid_rows: int32 [32], replicated, may hold values from 0 to 32767
- column_offset: int32 [1], replicated, may hold values from 0 to 32767
- uv_coords: int32 [2, 256, 8, 512], P(None, ('freq', 'facet')), may hold values from 0 to 255
- observed: bfloat16 [2, 256, 8, 512], P(None, ('freq', 'facet')), may hold values from -6 to 6
Outputs:
- image_residual: bfloat16 [16, 2, 512, 4096], P('facet', None, 'freq')
- residual_vis: bfloat16 [2, 256, 8, 512], P(None, ('freq', 'facet'))
The draws below stay inside these ranges and needn't reach their ends.
All inputs are finite; a program needn't handle non-finite values.
Results may differ from the reference program's by a relative error of at most 0.024.
Values may be sent and summed in bfloat16 or wider, within the bound.
A program may use at most 64 MiB of HBM per device.

```python
import math
import jax
import jax.numpy as jnp
from jax import lax

IMAGE = 32768
FACET_W = 4096
CONTRIB = 128
SUBGRID = 256
PATCH = 32
VIS_PATCH = 512
FACETS = 16
FACET_ROWS = 512
COL_STEP = 8
ROW_STEP = 64
SUBGRIDS = 32
SIDE = 8
STEP = 128
PERIOD = 256


def with_ends(drawn, own_key, least, high):
    index_at = [jax.random.randint(jax.random.fold_in(own_key, axis), (), 0, length) for axis, length in enumerate(drawn.shape)]
    widest = drawn.shape.index(max(drawn.shape))
    neighbour = index_at[:widest] + [(index_at[widest] + 1) % drawn.shape[widest]] + index_at[widest + 1:]
    return drawn.at[tuple(index_at)].set(least).at[tuple(neighbour)].set(high)


def levels(rng, shape, shards, smallest, high):
    loudness, own = 1.0, jax.random.fold_in(rng, 6)
    for dim, shards_of in shards:
        steps = jnp.exp(jax.random.uniform(jax.random.fold_in(own, dim), (shards_of,), jnp.float32, smallest / len(shards), high / len(shards)))
        loudness = loudness * jnp.repeat(steps, shape[dim] // shards_of).reshape([-1 if axis == dim else 1 for axis in range(len(shape))])
    return loudness


def normal_values(rng, shape, width, limit, split=(), held_as=jnp.bfloat16):
    array = width * jax.random.normal(rng, shape, jnp.float32)
    if split:
        array = array * levels(rng, shape, split, -0.22, 0.18)
    return jnp.clip(array, -limit, limit).astype(held_as)


def setup_inputs(seed: int = 0) -> dict:
    streams_of = jax.random.split(jax.random.key(seed), 7)
    return {
        "facet_image": normal_values(streams_of[0], (FACETS, 2, FACET_ROWS, FACET_W), 1.0, 6.0, ((0, 16), (2, 16))),
        "facet_offsets": with_ends(jax.random.randint(streams_of[1], (FACETS, 2), 0, IMAGE), jax.random.fold_in(streams_of[1], 1), 0, IMAGE - 1).astype(jnp.int32),
        "subgrid_rows": with_ends(jax.random.randint(streams_of[2], (SUBGRIDS,), 0, IMAGE), jax.random.fold_in(streams_of[2], 1), 0, IMAGE - 1).astype(jnp.int32),
        "column_offset": jax.random.randint(streams_of[3], (1,), 0, IMAGE).astype(jnp.int32),
        "uv_coords": with_ends(jax.random.randint(streams_of[4], (2, SUBGRIDS * SIDE, SIDE, VIS_PATCH), 0, PERIOD), jax.random.fold_in(streams_of[4], 1), 0, PERIOD - 1).astype(jnp.int32),
        "observed": normal_values(streams_of[5], (2, SUBGRIDS * SIDE, SIDE, VIS_PATCH), 1.0, 6.0, ((1, 256),)),
    }


TWO_PI = 2.0 * math.pi

def phases(product, modulus, direction):
    angles = product.astype(jnp.float32) * (direction * TWO_PI / modulus)
    return (jnp.cos(angles).astype(jnp.bfloat16), jnp.sin(angles).astype(jnp.bfloat16))

def complex_product(pattern, left_real, left_imag, right_real, right_imag):
    lr = left_real.astype(jnp.float32)
    li = left_imag.astype(jnp.float32)
    rr = right_real.astype(jnp.float32)
    ri = right_imag.astype(jnp.float32)
    real_part = jnp.einsum(pattern, lr, rr) - jnp.einsum(pattern, li, ri)
    imag_part = jnp.einsum(pattern, lr, ri) + jnp.einsum(pattern, li, rr)
    return (real_part, imag_part)

def row_table(starts, row_ids, offset):
    frequencies = (starts[:, None] + ROW_STEP * jnp.arange(CONTRIB, dtype=jnp.int32)[None, :]) % IMAGE
    places = (offset + row_ids) % IMAGE
    return phases(frequencies[:, :, None] * places[None, None, :] % IMAGE, IMAGE, -1.0)

def column_table(column, offset, extent):
    frequencies = (column + COL_STEP * jnp.arange(CONTRIB, dtype=jnp.int32)) % IMAGE
    places = (offset + jnp.arange(extent, dtype=jnp.int32)) % IMAGE
    return phases(frequencies[:, None] * places[None, :] % IMAGE, IMAGE, -1.0)

def spread_table(row_ids, offsets):
    columns = (STEP * jnp.arange(CONTRIB, dtype=jnp.int32)[None, :] + offsets[:, None]) % IMAGE
    return phases(row_ids[None, :, None] * columns[:, None, :] % IMAGE, IMAGE, 1.0)

def patch_table(coords):
    cell_ids = jnp.arange(PATCH, dtype=jnp.int32)
    return phases(cell_ids[:, None] * coords[..., None, :] % PERIOD, PERIOD, 1.0)

def predict_and_adjoint(grid_real, grid_imag, coords_u, coords_v, seen_real, seen_imag):
    patch_rows = grid_real.shape[0] // PATCH
    vis_count = coords_u.shape[-1]

    def to_patches(grid):
        return grid.reshape(patch_rows, PATCH, SIDE, PATCH).transpose(0, 2, 1, 3)
    eu_real, eu_imag = patch_table(coords_u)
    ev_real, ev_imag = patch_table(coords_v)
    inner_real, inner_imag = complex_product('bcrs,bcst->bcrt', to_patches(grid_real), to_patches(grid_imag), ev_real, ev_imag)
    model_real = lax.optimization_barrier(jnp.sum(eu_real * inner_real - eu_imag * inner_imag, axis=2)) * (1.0 / PATCH)
    model_imag = lax.optimization_barrier(jnp.sum(eu_real * inner_imag + eu_imag * inner_real, axis=2)) * (1.0 / PATCH)
    residual_real = (seen_real.astype(jnp.float32) - model_real).astype(jnp.bfloat16)
    residual_imag = (seen_imag.astype(jnp.float32) - model_imag).astype(jnp.bfloat16)
    wide_real = residual_real.astype(jnp.float32)[:, :, None, :]
    wide_imag = residual_imag.astype(jnp.float32)[:, :, None, :]
    weighted_real = (wide_real * eu_real + wide_imag * eu_imag).astype(jnp.bfloat16)
    weighted_imag = (wide_imag * eu_real - wide_real * eu_imag).astype(jnp.bfloat16)
    grid_back_real, grid_back_imag = complex_product('bcrt,bcst->bcrs', weighted_real, weighted_imag, ev_real, -ev_imag)
    factor = 1.0 / math.sqrt(vis_count)

    def from_patches(grid):
        return (grid * factor).astype(jnp.bfloat16).transpose(0, 2, 1, 3).reshape(patch_rows * PATCH, SUBGRID)
    return (residual_real, residual_imag, from_patches(grid_back_real), from_patches(grid_back_imag))

def reference(facet_image, facet_offsets, subgrid_rows, column_offset, uv_coords, observed):
    column = column_offset[0]
    scale_cols = 1.0 / math.sqrt(FACET_W)
    scale_rows = 1.0 / math.sqrt(FACET_ROWS)
    adjoint_scale = 1.0 / math.sqrt(SUBGRIDS * CONTRIB)
    final_scale = 1.0 / math.sqrt(CONTRIB)
    all_rows = jnp.arange(FACET_ROWS, dtype=jnp.int32)

    def facet_forward(inputs):
        facet_data, offset = inputs
        col_real, col_imag = column_table(column, offset[1], FACET_W)
        raw_real, raw_imag = complex_product('xy,ky->xk', facet_data[0], facet_data[1], col_real, col_imag)
        trans_real = (raw_real * scale_cols).astype(jnp.bfloat16)
        trans_imag = (raw_imag * scale_cols).astype(jnp.bfloat16)
        row_real, row_imag = row_table(subgrid_rows, all_rows, offset[0])
        sum_real, sum_imag = complex_product('jkx,xl->jkl', row_real, row_imag, trans_real, trans_imag)
        return (jnp.stack((sum_real, sum_imag), axis=1) * scale_rows).astype(jnp.bfloat16)
    contributions = lax.map(facet_forward, (facet_image, facet_offsets))
    grid_ids = jnp.arange(SUBGRID, dtype=jnp.int32)
    spread_real, spread_imag = spread_table(grid_ids, facet_offsets[:, 0])
    cols_real, cols_imag = spread_table(grid_ids, facet_offsets[:, 1])

    def subgrid_section(inputs):
        contrib, coords, seen = inputs
        part_real, part_imag = complex_product('frk,fkl->frl', spread_real, spread_imag, contrib[:, 0], contrib[:, 1])
        part_real = part_real.astype(jnp.bfloat16)
        part_imag = part_imag.astype(jnp.bfloat16)
        grid_real, grid_imag = complex_product('frl,fsl->rs', part_real, part_imag, cols_real, cols_imag)
        grid_real = (grid_real * (1.0 / CONTRIB)).astype(jnp.bfloat16)
        grid_imag = (grid_imag * (1.0 / CONTRIB)).astype(jnp.bfloat16)
        res_real, res_imag, back_real, back_imag = predict_and_adjoint(grid_real, grid_imag, coords[0], coords[1], seen[0], seen[1])
        narrow_real, narrow_imag = complex_product('rs,fsl->frl', back_real, back_imag, cols_real, -cols_imag)
        narrow_real = narrow_real.astype(jnp.bfloat16)
        narrow_imag = narrow_imag.astype(jnp.bfloat16)
        adj_real, adj_imag = complex_product('frk,frl->fkl', spread_real, -spread_imag, narrow_real, narrow_imag)
        adjoint = (jnp.stack((adj_real, adj_imag), axis=1) * (1.0 / SUBGRID)).astype(jnp.bfloat16)
        return (jnp.stack((res_real, res_imag), axis=0), adjoint)
    coords_all = uv_coords.reshape(2, SUBGRIDS, SIDE, SIDE, VIS_PATCH).transpose(1, 0, 2, 3, 4)
    seen_all = observed.reshape(2, SUBGRIDS, SIDE, SIDE, VIS_PATCH).transpose(1, 0, 2, 3, 4)
    residuals, adjoints = lax.map(subgrid_section, (contributions.transpose(1, 0, 2, 3, 4), coords_all, seen_all))
    residual_vis = residuals.transpose(1, 0, 2, 3, 4).reshape(2, SUBGRIDS * SIDE, SIDE, VIS_PATCH)

    def facet_adjoint(inputs):
        adjoint, offset = inputs
        row_real, row_imag = row_table(subgrid_rows, all_rows, offset[0])
        sum_real, sum_imag = complex_product('jkx,jkl->xl', row_real, -row_imag, adjoint[:, 0], adjoint[:, 1])
        back_real = (sum_real * adjoint_scale).astype(jnp.bfloat16)
        back_imag = (sum_imag * adjoint_scale).astype(jnp.bfloat16)
        col_real, col_imag = column_table(column, offset[1], FACET_W)
        out_real, out_imag = complex_product('xk,ky->xy', back_real, back_imag, col_real, -col_imag)
        return (jnp.stack((out_real, out_imag), axis=0) * final_scale).astype(jnp.bfloat16)
    image_residual = lax.map(facet_adjoint, (adjoints.transpose(1, 0, 2, 3, 4), facet_offsets))
    return (image_residual, residual_vis)
```

```python
import math

import jax
import jax.numpy as jnp
from jax import lax
from jax.experimental import pallas as pl
from jax.experimental.pallas import tpu as pltpu
from jax.sharding import PartitionSpec as P

IMAGE = 32768
CONTRIB = 128
SUBGRID = 256
PATCH = 32
SIDE = 8
PERIOD = 256
COL_STEP = 8
ROW_STEP = 64
STEP = 128
FACETS = 16
FREQS = 16
ROWS_DEV = 32
FACET_ROWS = FREQS * ROWS_DEV
FACET_W = 4096
SUBGRIDS = 32
OWN = 2
VIS = 512
LANES = 128
BLOCKS = FACET_W // LANES
PAIR = 2 * CONTRIB

TWO_PI = 2.0 * math.pi
MESH = pl.DeviceIdType.MESH
F32 = jnp.float32
BF16 = jnp.bfloat16


def iota(shape, dim):
    return lax.broadcasted_iota(jnp.int32, shape, dim)


def wrap(m):
    return m & (IMAGE - 1)


def cis(m, period=IMAGE):
    quarter = period // 4
    m = m & (period - 1)
    turn = lax.shift_right_logical(m + quarter // 2, int(math.log2(quarter)))
    rest = (m - turn * quarter).astype(F32) * (TWO_PI / period)
    sq = rest * rest
    sin = 1.0 / 120.0 + sq * (-1.0 / 5040.0 + sq * (1.0 / 362880.0))
    sin = rest + rest * (sq * (-1.0 / 6.0 + sq * sin))
    cos = 1.0 / 24.0 + sq * (-1.0 / 720.0 + sq * (1.0 / 40320.0))
    cos = 1.0 + sq * (-0.5 + sq * cos)
    odd = (turn & 1) == 1
    c = jnp.where(odd, sin, cos)
    s = jnp.where(odd, cos, sin)
    c = jnp.where(((turn + 1) & 2) == 2, -c, c)
    s = jnp.where((turn & 2) == 2, -s, s)
    return c, s


def cmul(a, b):
    return a[0] * b[0] - a[1] * b[1], a[0] * b[1] + a[1] * b[0]


def outer(fine, coarse):
    rows = [
        cmul(fine, (coarse[0][h : h + 1], coarse[1][h : h + 1])) for h in range(coarse[0].shape[0])
    ]
    return jnp.concatenate([r[0] for r in rows], 0), jnp.concatenate([r[1] for r in rows], 0)


def dot(a, b):
    return jnp.dot(a, b, preferred_element_type=F32)


def kernel(
    offs_s,
    starts_s,
    col_s,
    offs_v,
    facet_in,
    uv_in,
    seen_in,
    img_out,
    res_out,
    facet_v,
    uv_v,
    seen_v,
    wide,
    prod,
    col_w,
    back_w,
    tw_r,
    tw_i,
    row_t,
    row_h,
    spread_t,
    spread_h,
    grid_w,
    narrow_w,
    ph_r,
    ph_i,
    eu_r,
    eu_i,
    ev,
    quad,
    weigh,
    shifted,
    gath,
    send_b,
    recv_b,
    send_c,
    recv_c,
    send_d,
    recv_d,
    in_sem,
    out_sem,
    tx_sem,
    rx_sem,
):
    f = lax.axis_index("facet")
    q = lax.axis_index("freq")

    load = pltpu.make_async_copy(facet_in, facet_v, in_sem.at[0])
    load.start()
    load_uv = pltpu.make_async_copy(uv_in, uv_v, in_sem.at[1])
    load_uv.start()
    load_seen = pltpu.make_async_copy(seen_in, seen_v, in_sem.at[2])
    load_seen.start()

    barrier = pltpu.get_barrier_semaphore()
    for i in range(1, FACETS):
        pl.semaphore_signal(
            barrier, inc=1, device_id={"facet": lax.rem(f + i, FACETS)}, device_id_type=MESH
        )
    for i in range(1, FREQS):
        pl.semaphore_signal(
            barrier, inc=1, device_id={"freq": lax.rem(q + i, FREQS)}, device_id_type=MESH
        )

    a = offs_s[f, 0]
    b = offs_s[f, 1]
    column = col_s[0]
    start0 = starts_s[OWN * q]
    start1 = starts_s[OWN * q + 1]

    def exchange(stage, axis, me, count, src, dst):
        copies = []
        for i in range(1, count):
            peer = lax.rem(me + i, count)
            copies.append(
                pltpu.make_async_remote_copy(
                    src_ref=src(peer),
                    dst_ref=dst.at[me],
                    send_sem=tx_sem.at[stage, i],
                    recv_sem=rx_sem.at[stage, i],
                    device_id={axis: peer},
                    device_id_type=MESH,
                )
            )
        for copy in copies:
            copy.start()
        return copies

    freq_l = wrap(column + COL_STEP * iota((8, LANES), 1))
    fine = cis(freq_l * iota((8, LANES), 0))
    freq_h = wrap(column + COL_STEP * iota((16, LANES), 1))
    coarse = cis(freq_h * (8 * iota((16, LANES), 0)))
    tr, ti = outer(fine, coarse)
    ti = -ti
    col_w[0:LANES, 0:LANES] = tr.astype(BF16)
    col_w[0:LANES, LANES:] = ti.astype(BF16)
    col_w[LANES:, 0:LANES] = (-ti).astype(BF16)
    col_w[LANES:, LANES:] = tr.astype(BF16)
    freq_b = wrap(column + COL_STEP * iota((BLOCKS, LANES), 1))
    wr, wi = cis(freq_b * wrap(b + LANES * iota((BLOCKS, LANES), 0)))
    tw_r[...] = wr
    tw_i[...] = wi

    load.wait()
    for y in range(BLOCKS):
        rows = slice(ROWS_DEV * y, ROWS_DEV * (y + 1))
        lanes = slice(LANES * y, LANES * (y + 1))
        wide[rows, 0:LANES] = facet_v[0:ROWS_DEV, lanes]
        wide[rows, LANES:] = facet_v[ROWS_DEV:, lanes]
    prod[...] = dot(wide[...], col_w[...])
    acc_r = jnp.zeros((ROWS_DEV, LANES), F32)
    acc_i = jnp.zeros((ROWS_DEV, LANES), F32)
    for y in range(BLOCKS):
        rows = slice(ROWS_DEV * y, ROWS_DEV * (y + 1))
        dr, di = prod[rows, 0:LANES], prod[rows, LANES:]
        cr, ci = tw_r[y : y + 1, :], tw_i[y : y + 1, :]
        acc_r += dr * cr + di * ci
        acc_i += di * cr - dr * ci
    transformed = jnp.concatenate([acc_r, acc_i], 1) * (1.0 / math.sqrt(FACET_W))
    gath[q] = transformed.astype(BF16)

    pl.semaphore_wait(barrier, FACETS - 1 + FREQS - 1)
    copies_a = exchange(0, "freq", q, FREQS, lambda peer: gath.at[q], gath)

    place = wrap(a + iota((8, FACET_ROWS), 1))
    coarse = cis(8 * ROW_STEP * iota((16, FACET_ROWS), 0) * wrap(a + iota((16, FACET_ROWS), 1)))
    for j, start in enumerate((start0, start1)):
        fine = cis(wrap(start + ROW_STEP * iota((8, FACET_ROWS), 0)) * place)
        rr, ri = outer(fine, coarse)
        row_t[CONTRIB * j : CONTRIB * (j + 1), :] = rr.astype(BF16)
        row_t[PAIR + CONTRIB * j : PAIR + CONTRIB * (j + 1), :] = (-ri).astype(BF16)

    lane_k = iota((8, CONTRIB), 1)
    fine = cis(iota((8, CONTRIB), 0) * wrap(STEP * lane_k + a))
    coarse = cis(8 * iota((32, CONTRIB), 0) * wrap(STEP * iota((32, CONTRIB), 1) + a))
    sr, si = outer(fine, coarse)
    spread_t[0:SUBGRID, :] = sr.astype(BF16)
    spread_t[SUBGRID:, :] = si.astype(BF16)

    fine = cis(STEP * iota((8, SUBGRID), 0) * iota((8, SUBGRID), 1))
    coarse = cis(8 * STEP * iota((16, SUBGRID), 0) * iota((16, SUBGRID), 1))
    gr, gi = outer(fine, coarse)
    grid_w[0:CONTRIB, 0:SUBGRID] = gr.astype(BF16)
    grid_w[0:CONTRIB, SUBGRID:] = gi.astype(BF16)
    grid_w[CONTRIB:, 0:SUBGRID] = (-gi).astype(BF16)
    grid_w[CONTRIB:, SUBGRID:] = gr.astype(BF16)

    shift_b = jnp.broadcast_to(offs_v[:, 1:2], (FACETS, SUBGRID))
    pr, pi = cis(iota((FACETS, SUBGRID), 1) * shift_b)
    ph_r[...] = pr
    ph_i[...] = pi

    for copy in copies_a:
        copy.wait_recv()
    rows_all = gath[...].reshape(FACET_ROWS, PAIR)
    both = dot(row_t[...], rows_all)
    cr = both[0:PAIR, 0:CONTRIB] - both[PAIR:, CONTRIB:]
    ci = both[0:PAIR, CONTRIB:] + both[PAIR:, 0:CONTRIB]
    contrib = (jnp.concatenate([cr, ci], 1) * (1.0 / math.sqrt(FACET_ROWS))).astype(BF16)
    for j in range(OWN):
        both = dot(spread_t[...], contrib[CONTRIB * j : CONTRIB * (j + 1), :])
        sr = both[0:SUBGRID, 0:CONTRIB] - both[SUBGRID:, CONTRIB:]
        si = both[0:SUBGRID, CONTRIB:] + both[SUBGRID:, 0:CONTRIB]
        part = jnp.concatenate([sr, si], 1).astype(BF16)
        send_b[SIDE * j : SIDE * (j + 1)] = part.reshape(SIDE, PATCH, PAIR)
    copies_b = exchange(1, "facet", f, FACETS, lambda peer: send_b.at[peer], recv_b)
    recv_b[f] = send_b[f]

    load_uv.wait()
    load_seen.wait()

    def patch_rows(coords):
        cell = iota((8, VIS), 0)
        by8 = cis(8 * coords, PERIOD)
        by16 = cis(16 * coords, PERIOD)
        for c in range(SIDE):
            row = jnp.broadcast_to(coords[c : c + 1], (8, VIS))
            low = cis(cell * row, PERIOD)
            mid = cmul(low, (by8[0][c : c + 1], by8[1][c : c + 1]))
            half = (jnp.concatenate([low[0], mid[0]], 0), jnp.concatenate([low[1], mid[1]], 0))
            high = cmul(half, (by16[0][c : c + 1], by16[1][c : c + 1]))
            yield (
                c,
                jnp.concatenate([half[0], high[0]], 0),
                jnp.concatenate([half[1], high[1]], 0),
            )

    for c, er, ei in patch_rows(uv_v[0:SIDE, :]):
        eu_r[PATCH * c : PATCH * (c + 1), :] = er
        eu_i[PATCH * c : PATCH * (c + 1), :] = ei
    for c, er, ei in patch_rows(uv_v[SIDE:, :]):
        ev[PATCH * c : PATCH * (c + 1), :] = er.astype(BF16)
        ev[SUBGRID + PATCH * c : SUBGRID + PATCH * (c + 1), :] = ei.astype(BF16)

    fine = cis(STEP * iota((8, CONTRIB), 0) * lane_k)
    coarse = cis(8 * STEP * iota((32, CONTRIB), 0) * iota((32, CONTRIB), 1))
    nr, ni = outer(fine, coarse)
    narrow_w[0:SUBGRID, 0:CONTRIB] = nr.astype(BF16)
    narrow_w[0:SUBGRID, CONTRIB:] = (-ni).astype(BF16)
    narrow_w[SUBGRID:, 0:CONTRIB] = ni.astype(BF16)
    narrow_w[SUBGRID:, CONTRIB:] = nr.astype(BF16)

    fine = cis(wrap(STEP * iota((8, SUBGRID), 0) + a) * iota((8, SUBGRID), 1))
    coarse = cis(8 * STEP * iota((16, SUBGRID), 0) * iota((16, SUBGRID), 1))
    hr, hi = outer(fine, coarse)
    spread_h[0:CONTRIB, :] = hr.astype(BF16)
    spread_h[CONTRIB:, :] = (-hi).astype(BF16)

    def own_freq(rows):
        lane = iota((rows, PAIR), 1)
        start = jnp.where(lane < CONTRIB, start0, start1)
        return wrap(start + ROW_STEP * (lane & (CONTRIB - 1)))

    fine = cis(own_freq(8) * wrap(a + iota((8, PAIR), 0)))
    coarse = cis(own_freq(FACET_ROWS // 8) * (8 * iota((FACET_ROWS // 8, PAIR), 0)))
    hr, hi = outer(fine, coarse)
    row_h[0:FACET_ROWS, :] = hr.astype(BF16)
    row_h[FACET_ROWS:, :] = hi.astype(BF16)

    fine = cis(wrap(column + COL_STEP * iota((8, LANES), 0)) * iota((8, LANES), 1))
    coarse = cis(8 * COL_STEP * iota((16, LANES), 0) * iota((16, LANES), 1))
    br, bi = outer(fine, coarse)
    back_w[0:LANES, 0:LANES] = br.astype(BF16)
    back_w[0:LANES, LANES:] = bi.astype(BF16)
    back_w[LANES:, 0:LANES] = (-bi).astype(BF16)
    back_w[LANES:, LANES:] = br.astype(BF16)

    for copy in copies_b:
        copy.wait_recv()
    quad[...] = dot(recv_b[...].reshape(FACETS * PATCH, PAIR), grid_w[...])
    grid_r = jnp.zeros((PATCH, SUBGRID), F32)
    grid_i = jnp.zeros((PATCH, SUBGRID), F32)
    for g in range(FACETS):
        rows = slice(PATCH * g, PATCH * (g + 1))
        qr, qi = quad[rows, 0:SUBGRID], quad[rows, SUBGRID:]
        pr, pi = ph_r[g : g + 1, :], ph_i[g : g + 1, :]
        grid_r += qr * pr - qi * pi
        grid_i += qr * pi + qi * pr
    grid_r = grid_r * (1.0 / CONTRIB)
    grid_i = grid_i * (1.0 / CONTRIB)

    patch_of = lax.shift_right_logical(iota((PATCH, SUBGRID), 1), 5)
    for c in range(SIDE):
        mine = patch_of == c
        gr = jnp.where(mine, grid_r, 0.0)
        gi = jnp.where(mine, grid_i, 0.0)
        rows = slice(PATCH * c, PATCH * (c + 1))
        low = slice(SUBGRID + PATCH * c, SUBGRID + PATCH * (c + 1))
        weigh[rows, 0:SUBGRID] = gr.astype(BF16)
        weigh[rows, SUBGRID:] = (-gi).astype(BF16)
        weigh[low, 0:SUBGRID] = gi.astype(BF16)
        weigh[low, SUBGRID:] = gr.astype(BF16)
    quad[...] = dot(weigh[...], ev[...])
    models_r, models_i = [], []
    for c in range(SIDE):
        rows = slice(PATCH * c, PATCH * (c + 1))
        low = slice(SUBGRID + PATCH * c, SUBGRID + PATCH * (c + 1))
        inner_r, inner_i = quad[rows, :], quad[low, :]
        ur, ui = eu_r[rows, :], eu_i[rows, :]
        models_r.append(jnp.sum(ur * inner_r - ui * inner_i, axis=0, keepdims=True))
        models_i.append(jnp.sum(ur * inner_i + ui * inner_r, axis=0, keepdims=True))
    model = jnp.concatenate(models_r + models_i, 0) * (1.0 / PATCH)
    residual = (seen_v[...].astype(F32) - model).astype(BF16)
    res_out[...] = residual
    residual = residual.astype(F32)
    for c in range(SIDE):
        rows = slice(PATCH * c, PATCH * (c + 1))
        low = slice(SUBGRID + PATCH * c, SUBGRID + PATCH * (c + 1))
        rr, ri = residual[c : c + 1, :], residual[SIDE + c : SIDE + c + 1, :]
        ur, ui = eu_r[rows, :], eu_i[rows, :]
        weigh[rows, :] = (rr * ur + ri * ui).astype(BF16)
        weigh[low, :] = (ri * ur - rr * ui).astype(BF16)
    quad[...] = lax.dot_general(
        weigh[...], ev[...], (((1,), (1,)), ((), ())), preferred_element_type=F32
    )
    back_r = jnp.zeros((PATCH, SUBGRID), F32)
    back_i = jnp.zeros((PATCH, SUBGRID), F32)
    for c in range(SIDE):
        mine = patch_of == c
        rows = slice(PATCH * c, PATCH * (c + 1))
        low = slice(SUBGRID + PATCH * c, SUBGRID + PATCH * (c + 1))
        back_r = jnp.where(mine, quad[rows, 0:SUBGRID] + quad[low, SUBGRID:], back_r)
        back_i = jnp.where(mine, quad[low, 0:SUBGRID] - quad[rows, SUBGRID:], back_i)
    back_r = back_r * (1.0 / math.sqrt(VIS))
    back_i = back_i * (1.0 / math.sqrt(VIS))

    for g in range(FACETS):
        rows = slice(PATCH * g, PATCH * (g + 1))
        pr, pi = ph_r[g : g + 1, :], ph_i[g : g + 1, :]
        shifted[rows, 0:SUBGRID] = (back_r * pr + back_i * pi).astype(BF16)
        shifted[rows, SUBGRID:] = (back_i * pr - back_r * pi).astype(BF16)
    narrowed = dot(shifted[...], narrow_w[...]).astype(BF16)
    send_c[...] = narrowed.reshape(FACETS, PATCH, PAIR)
    copies_c = exchange(2, "facet", f, FACETS, lambda peer: send_c.at[peer], recv_c)
    recv_c[f] = send_c[f]

    for copy in copies_c:
        copy.wait_recv()
    came_back = recv_c[...].reshape(OWN, SUBGRID, PAIR)
    adjoint = []
    for j in range(OWN):
        both = dot(spread_h[...], came_back[j])
        ar = both[0:CONTRIB, 0:CONTRIB] - both[CONTRIB:, CONTRIB:]
        ai = both[0:CONTRIB, CONTRIB:] + both[CONTRIB:, 0:CONTRIB]
        adjoint.append((jnp.concatenate([ar, ai], 1) * (1.0 / SUBGRID)).astype(BF16))
    both = dot(row_h[...], jnp.concatenate(adjoint, 0))
    rr = both[0:FACET_ROWS, 0:CONTRIB] - both[FACET_ROWS:, CONTRIB:]
    ri = both[0:FACET_ROWS, CONTRIB:] + both[FACET_ROWS:, 0:CONTRIB]
    rows_sum = jnp.concatenate([rr, ri], 1).astype(BF16)
    send_d[...] = rows_sum.reshape(FREQS, ROWS_DEV, PAIR)
    copies_d = exchange(3, "freq", q, FREQS, lambda peer: send_d.at[peer], recv_d)
    recv_d[q] = send_d[q]

    for copy in copies_d:
        copy.wait_recv()
    total = jnp.zeros((ROWS_DEV, PAIR), F32)
    for g in range(FREQS):
        total += recv_d[g].astype(F32)
    total = total * (1.0 / (math.sqrt(SUBGRIDS * CONTRIB) * math.sqrt(CONTRIB)))
    tot_r, tot_i = total[:, 0:CONTRIB], total[:, CONTRIB:]
    for y in range(BLOCKS):
        rows = slice(ROWS_DEV * y, ROWS_DEV * (y + 1))
        cr, ci = tw_r[y : y + 1, :], tw_i[y : y + 1, :]
        wide[rows, 0:LANES] = (tot_r * cr - tot_i * ci).astype(BF16)
        wide[rows, LANES:] = (tot_r * ci + tot_i * cr).astype(BF16)
    prod[...] = dot(wide[...], back_w[...])
    for y in range(BLOCKS):
        rows = slice(ROWS_DEV * y, ROWS_DEV * (y + 1))
        lanes = slice(LANES * y, LANES * (y + 1))
        facet_v[0:ROWS_DEV, lanes] = prod[rows, 0:LANES].astype(BF16)
        facet_v[ROWS_DEV:, lanes] = prod[rows, LANES:].astype(BF16)
    store = pltpu.make_async_copy(facet_v, img_out, out_sem.at[0])
    store.start()
    for copies in (copies_a, copies_b, copies_c, copies_d):
        for copy in copies:
            copy.wait_send()
    store.wait()


def on_device(facet_image, facet_offsets, subgrid_rows, column_offset, uv_coords, observed):
    smem = pl.BlockSpec(memory_space=pltpu.SMEM)
    vmem = pl.BlockSpec(memory_space=pltpu.VMEM)
    hbm = pl.BlockSpec(memory_space=pl.ANY)
    chunk = pltpu.VMEM((16, 32, PAIR), BF16)
    image, residual = pl.pallas_call(
        kernel,
        out_shape=(
            jax.ShapeDtypeStruct((2 * ROWS_DEV, FACET_W), BF16),
            jax.ShapeDtypeStruct((2 * SIDE, VIS), BF16),
        ),
        in_specs=[smem, smem, smem, vmem, hbm, hbm, hbm],
        out_specs=(hbm, vmem),
        scratch_shapes=[
            pltpu.VMEM((2 * ROWS_DEV, FACET_W), BF16),
            pltpu.VMEM((2 * SIDE, VIS), jnp.int32),
            pltpu.VMEM((2 * SIDE, VIS), BF16),
            pltpu.VMEM((BLOCKS * ROWS_DEV, PAIR), BF16),
            pltpu.VMEM((BLOCKS * ROWS_DEV, PAIR), F32),
            pltpu.VMEM((PAIR, PAIR), BF16),
            pltpu.VMEM((PAIR, PAIR), BF16),
            pltpu.VMEM((BLOCKS, LANES), F32),
            pltpu.VMEM((BLOCKS, LANES), F32),
            pltpu.VMEM((2 * PAIR, FACET_ROWS), BF16),
            pltpu.VMEM((2 * FACET_ROWS, PAIR), BF16),
            pltpu.VMEM((2 * SUBGRID, CONTRIB), BF16),
            pltpu.VMEM((2 * CONTRIB, SUBGRID), BF16),
            pltpu.VMEM((PAIR, 2 * SUBGRID), BF16),
            pltpu.VMEM((2 * SUBGRID, PAIR), BF16),
            pltpu.VMEM((FACETS, SUBGRID), F32),
            pltpu.VMEM((FACETS, SUBGRID), F32),
            pltpu.VMEM((SUBGRID, VIS), F32),
            pltpu.VMEM((SUBGRID, VIS), F32),
            pltpu.VMEM((2 * SUBGRID, VIS), BF16),
            pltpu.VMEM((2 * SUBGRID, 2 * SUBGRID), F32),
            pltpu.VMEM((2 * SUBGRID, 2 * SUBGRID), BF16),
            pltpu.VMEM((2 * SUBGRID, 2 * SUBGRID), BF16),
            chunk,
            chunk,
            chunk,
            chunk,
            chunk,
            chunk,
            chunk,
            pltpu.SemaphoreType.DMA((3,)),
            pltpu.SemaphoreType.DMA((1,)),
            pltpu.SemaphoreType.DMA((4, 16)),
            pltpu.SemaphoreType.DMA((4, 16)),
        ],
        compiler_params=pltpu.CompilerParams(
            collective_id=0, has_side_effects=True, vmem_limit_bytes=40 * 1024 * 1024
        ),
    )(
        facet_offsets,
        subgrid_rows,
        column_offset,
        facet_offsets,
        facet_image.reshape(2 * ROWS_DEV, FACET_W),
        uv_coords.reshape(2 * SIDE, VIS),
        observed.reshape(2 * SIDE, VIS),
    )
    return (
        image.reshape(1, 2, ROWS_DEV, FACET_W),
        residual.reshape(2, 1, SIDE, VIS),
    )


def solution(mesh):
    return jax.shard_map(
        on_device,
        mesh=mesh,
        in_specs=(
            P("facet", None, "freq", None),
            P(),
            P(),
            P(),
            P(None, ("freq", "facet"), None, None),
            P(None, ("freq", "facet"), None, None),
        ),
        out_specs=(P("facet", None, "freq", None), P(None, ("freq", "facet"), None, None)),
        check_vma=False,
    )
```

```python
import math

import jax
import jax.numpy as jnp
from jax import lax
from jax.experimental import pallas as pl
from jax.experimental.pallas import tpu as pltpu
from jax.sharding import PartitionSpec as P

IMAGE = 32768
CONTRIB = 128
SUBGRID = 256
PATCH = 32
SIDE = 8
PERIOD = 256
COL_STEP = 8
ROW_STEP = 64
STEP = 128
FACETS = 16
FREQS = 16
ROWS_DEV = 32
FACET_ROWS = FREQS * ROWS_DEV
FACET_W = 4096
SUBGRIDS = 32
OWN = 2
VIS = 512
LANES = 128
BLOCKS = FACET_W // LANES
PAIR = 2 * CONTRIB
PARTS = 4

TWO_PI = 2.0 * math.pi
MESH = pl.DeviceIdType.MESH
F32 = jnp.float32
BF16 = jnp.bfloat16


def ring_hops(step, size):
    return min(step, size - step)


FACET_STEPS = sorted(
    [(x, z) for x in range(4) for z in range(4) if x or z],
    key=lambda s: -ring_hops(s[0], 4) - 2 * ring_hops(s[1], 4),
)
FREQ_STEPS = sorted(
    [(z, y, c) for z in range(2) for y in range(4) for c in range(2) if z or y or c],
    key=lambda s: -s[0] - ring_hops(s[1], 4),
)


def facet_peer(f, step):
    return lax.rem(f // 4 + step[0], 4) * 4 + lax.rem(lax.rem(f, 4) + step[1], 4)


def freq_peer(q, step):
    z, y, c = q // 8, lax.rem(q // 2, 4), lax.rem(q, 2)
    return (lax.rem(z + step[0], 2) * 4 + lax.rem(y + step[1], 4)) * 2 + lax.rem(c + step[2], 2)


def iota(shape, dim):
    return lax.broadcasted_iota(jnp.int32, shape, dim)


def wrap(m):
    return m & (IMAGE - 1)


def cis(m, period=IMAGE):
    quarter = period // 4
    m = m & (period - 1)
    turn = lax.shift_right_logical(m + quarter // 2, int(math.log2(quarter)))
    rest = (m - turn * quarter).astype(F32) * (TWO_PI / period)
    sq = rest * rest
    sin = 1.0 / 120.0 + sq * (-1.0 / 5040.0 + sq * (1.0 / 362880.0))
    sin = rest + rest * (sq * (-1.0 / 6.0 + sq * sin))
    cos = 1.0 / 24.0 + sq * (-1.0 / 720.0 + sq * (1.0 / 40320.0))
    cos = 1.0 + sq * (-0.5 + sq * cos)
    odd = (turn & 1) == 1
    c = jnp.where(odd, sin, cos)
    s = jnp.where(odd, cos, sin)
    c = jnp.where(((turn + 1) & 2) == 2, -c, c)
    s = jnp.where((turn & 2) == 2, -s, s)
    return c, s


def cmul(a, b):
    return a[0] * b[0] - a[1] * b[1], a[0] * b[1] + a[1] * b[0]


def outer(fine, coarse):
    rows = [
        cmul(fine, (coarse[0][h : h + 1], coarse[1][h : h + 1])) for h in range(coarse[0].shape[0])
    ]
    return jnp.concatenate([r[0] for r in rows], 0), jnp.concatenate([r[1] for r in rows], 0)


def dot(a, b):
    return jnp.dot(a, b, preferred_element_type=F32)


def kernel(
    offs_in,
    starts_in,
    col_s,
    facet_in,
    uv_in,
    seen_in,
    total_out,
    tw_r,
    tw_i,
    back_w,
    res_out,
    offs_s,
    starts_s,
    facet_v,
    uv_v,
    seen_v,
    wide,
    prod,
    col_w,
    row_t,
    row_h,
    spread_t,
    spread_h,
    grid_w,
    narrow_w,
    ph_r,
    ph_i,
    eu_r,
    eu_i,
    ev,
    quad,
    weigh,
    shifted,
    gath,
    send_b,
    recv_b,
    send_c,
    recv_c,
    send_d,
    recv_d,
    in_sem,
    tx_sem,
    rx_sem,
):
    f = lax.axis_index("facet")
    q = lax.axis_index("freq")

    loads = [
        pltpu.make_async_copy(src, dst, in_sem.at[3 + i])
        for i, (src, dst) in enumerate(
            ((offs_in, offs_s), (starts_in, starts_s))
        )
    ]
    for copy in loads:
        copy.start()
    load = pltpu.make_async_copy(facet_in, facet_v, in_sem.at[0])
    load.start()
    load_uv = pltpu.make_async_copy(uv_in, uv_v, in_sem.at[1])
    load_uv.start()
    load_seen = pltpu.make_async_copy(seen_in, seen_v, in_sem.at[2])
    load_seen.start()

    barrier = pltpu.get_barrier_semaphore()
    facet_peers = [facet_peer(f, step) for step in FACET_STEPS]
    freq_peers = [freq_peer(q, step) for step in FREQ_STEPS]
    for peer in facet_peers:
        pl.semaphore_signal(barrier, inc=1, device_id={"facet": peer}, device_id_type=MESH)
    for peer in freq_peers:
        pl.semaphore_signal(barrier, inc=1, device_id={"freq": peer}, device_id_type=MESH)

    for copy in loads:
        copy.wait()
    a = offs_s[0, f]
    b = offs_s[1, f]
    column = col_s[0]
    start0 = starts_s[OWN * q]
    start1 = starts_s[OWN * q + 1]

    def exchange(stage, axis, me, peers, src, dst):
        copies = []
        for i, peer in enumerate(peers):
            copies.append(
                pltpu.make_async_remote_copy(
                    src_ref=src(peer),
                    dst_ref=dst.at[me],
                    send_sem=tx_sem.at[stage, i],
                    recv_sem=rx_sem.at[stage, i],
                    device_id={axis: peer},
                    device_id_type=MESH,
                )
            )
        for copy in copies:
            copy.start()
        return copies

    freq_l = wrap(column + COL_STEP * iota((8, LANES), 1))
    fine = cis(freq_l * iota((8, LANES), 0))
    freq_h = wrap(column + COL_STEP * iota((16, LANES), 1))
    coarse = cis(freq_h * (8 * iota((16, LANES), 0)))
    tr, ti = outer(fine, coarse)
    ti = -ti
    col_w[0:LANES, 0:LANES] = tr.astype(BF16)
    col_w[0:LANES, LANES:] = ti.astype(BF16)
    col_w[LANES:, 0:LANES] = (-ti).astype(BF16)
    col_w[LANES:, LANES:] = tr.astype(BF16)
    freq_b = wrap(column + COL_STEP * iota((BLOCKS, LANES), 1))
    wr, wi = cis(freq_b * wrap(b + LANES * iota((BLOCKS, LANES), 0)))
    tw_r[...] = wr
    tw_i[...] = wi

    load.wait()
    for y in range(BLOCKS):
        rows = slice(ROWS_DEV * y, ROWS_DEV * (y + 1))
        lanes = slice(LANES * y, LANES * (y + 1))
        wide[rows, 0:LANES] = facet_v[0:ROWS_DEV, lanes]
        wide[rows, LANES:] = facet_v[ROWS_DEV:, lanes]
    prod[...] = dot(wide[...], col_w[...])
    acc_r = jnp.zeros((ROWS_DEV, LANES), F32)
    acc_i = jnp.zeros((ROWS_DEV, LANES), F32)
    for y in range(BLOCKS):
        rows = slice(ROWS_DEV * y, ROWS_DEV * (y + 1))
        dr, di = prod[rows, 0:LANES], prod[rows, LANES:]
        cr, ci = tw_r[y : y + 1, :], tw_i[y : y + 1, :]
        acc_r += dr * cr + di * ci
        acc_i += di * cr - dr * ci
    transformed = jnp.concatenate([acc_r, acc_i], 1) * (1.0 / math.sqrt(FACET_W))
    gath[q] = transformed.astype(BF16)

    pl.semaphore_wait(barrier, FACETS - 1 + FREQS - 1)
    copies_a = exchange(0, "freq", q, freq_peers, lambda peer: gath.at[q], gath)

    place = wrap(a + iota((8, FACET_ROWS), 1))
    coarse = cis(8 * ROW_STEP * iota((16, FACET_ROWS), 0) * wrap(a + iota((16, FACET_ROWS), 1)))
    for j, start in enumerate((start0, start1)):
        fine = cis(wrap(start + ROW_STEP * iota((8, FACET_ROWS), 0)) * place)
        rr, ri = outer(fine, coarse)
        row_t[CONTRIB * j : CONTRIB * (j + 1), :] = rr.astype(BF16)
        row_t[PAIR + CONTRIB * j : PAIR + CONTRIB * (j + 1), :] = (-ri).astype(BF16)

    lane_k = iota((8, CONTRIB), 1)
    fine = cis(iota((8, CONTRIB), 0) * wrap(STEP * lane_k + a))
    coarse = cis(8 * iota((32, CONTRIB), 0) * wrap(STEP * iota((32, CONTRIB), 1) + a))
    sr, si = outer(fine, coarse)
    spread_t[0:SUBGRID, :] = sr.astype(BF16)
    spread_t[SUBGRID:, :] = si.astype(BF16)

    fine = cis(STEP * iota((8, SUBGRID), 0) * iota((8, SUBGRID), 1))
    coarse = cis(8 * STEP * iota((16, SUBGRID), 0) * iota((16, SUBGRID), 1))
    gr, gi = outer(fine, coarse)
    grid_w[0:CONTRIB, 0:SUBGRID] = gr.astype(BF16)
    grid_w[0:CONTRIB, SUBGRID:] = gi.astype(BF16)
    grid_w[CONTRIB:, 0:SUBGRID] = (-gi).astype(BF16)
    grid_w[CONTRIB:, SUBGRID:] = gr.astype(BF16)

    shift_b = jnp.concatenate(
        [jnp.full((1, SUBGRID), offs_s[1, g], jnp.int32) for g in range(FACETS)], 0
    )
    pr, pi = cis(iota((FACETS, SUBGRID), 1) * shift_b)
    ph_r[...] = pr
    ph_i[...] = pi

    for copy in copies_a:
        copy.wait_recv()
    rows_all = gath[...].reshape(FACET_ROWS, PAIR)
    both = dot(row_t[...], rows_all)
    cr = both[0:PAIR, 0:CONTRIB] - both[PAIR:, CONTRIB:]
    ci = both[0:PAIR, CONTRIB:] + both[PAIR:, 0:CONTRIB]
    contrib = (jnp.concatenate([cr, ci], 1) * (1.0 / math.sqrt(FACET_ROWS))).astype(BF16)
    for j in range(OWN):
        both = dot(spread_t[...], contrib[CONTRIB * j : CONTRIB * (j + 1), :])
        sr = both[0:SUBGRID, 0:CONTRIB] - both[SUBGRID:, CONTRIB:]
        si = both[0:SUBGRID, CONTRIB:] + both[SUBGRID:, 0:CONTRIB]
        part = jnp.concatenate([sr, si], 1).astype(BF16)
        send_b[SIDE * j : SIDE * (j + 1)] = part.reshape(SIDE, PATCH, PAIR)
    copies_b = exchange(1, "facet", f, facet_peers, lambda peer: send_b.at[peer], recv_b)
    recv_b[f] = send_b[f]

    load_uv.wait()
    load_seen.wait()

    def patch_rows(coords):
        cell = iota((8, VIS), 0)
        by8 = cis(8 * coords, PERIOD)
        by16 = cis(16 * coords, PERIOD)
        for c in range(SIDE):
            row = jnp.broadcast_to(coords[c : c + 1], (8, VIS))
            low = cis(cell * row, PERIOD)
            mid = cmul(low, (by8[0][c : c + 1], by8[1][c : c + 1]))
            half = (jnp.concatenate([low[0], mid[0]], 0), jnp.concatenate([low[1], mid[1]], 0))
            high = cmul(half, (by16[0][c : c + 1], by16[1][c : c + 1]))
            yield (
                c,
                jnp.concatenate([half[0], high[0]], 0),
                jnp.concatenate([half[1], high[1]], 0),
            )

    for c, er, ei in patch_rows(uv_v[0:SIDE, :]):
        eu_r[PATCH * c : PATCH * (c + 1), :] = er
        eu_i[PATCH * c : PATCH * (c + 1), :] = ei
    for c, er, ei in patch_rows(uv_v[SIDE:, :]):
        ev[PATCH * c : PATCH * (c + 1), :] = er.astype(BF16)
        ev[SUBGRID + PATCH * c : SUBGRID + PATCH * (c + 1), :] = ei.astype(BF16)

    fine = cis(STEP * iota((8, CONTRIB), 0) * lane_k)
    coarse = cis(8 * STEP * iota((32, CONTRIB), 0) * iota((32, CONTRIB), 1))
    nr, ni = outer(fine, coarse)
    narrow_w[0:SUBGRID, 0:CONTRIB] = nr.astype(BF16)
    narrow_w[0:SUBGRID, CONTRIB:] = (-ni).astype(BF16)
    narrow_w[SUBGRID:, 0:CONTRIB] = ni.astype(BF16)
    narrow_w[SUBGRID:, CONTRIB:] = nr.astype(BF16)

    fine = cis(wrap(STEP * iota((8, SUBGRID), 0) + a) * iota((8, SUBGRID), 1))
    coarse = cis(8 * STEP * iota((16, SUBGRID), 0) * iota((16, SUBGRID), 1))
    hr, hi = outer(fine, coarse)
    spread_h[0:CONTRIB, :] = hr.astype(BF16)
    spread_h[CONTRIB:, :] = (-hi).astype(BF16)

    def own_freq(rows):
        lane = iota((rows, PAIR), 1)
        start = jnp.where(lane < CONTRIB, start0, start1)
        return wrap(start + ROW_STEP * (lane & (CONTRIB - 1)))

    fine = cis(own_freq(8) * wrap(a + iota((8, PAIR), 0)))
    coarse = cis(own_freq(FACET_ROWS // 8) * (8 * iota((FACET_ROWS // 8, PAIR), 0)))
    hr, hi = outer(fine, coarse)
    row_h[0:FACET_ROWS, :] = hr.astype(BF16)
    row_h[FACET_ROWS:, :] = hi.astype(BF16)

    fine = cis(wrap(column + COL_STEP * iota((8, LANES), 0)) * iota((8, LANES), 1))
    coarse = cis(8 * COL_STEP * iota((16, LANES), 0) * iota((16, LANES), 1))
    br, bi = outer(fine, coarse)
    back_w[0:LANES, 0:LANES] = br.astype(BF16)
    back_w[0:LANES, LANES:] = bi.astype(BF16)
    back_w[LANES:, 0:LANES] = (-bi).astype(BF16)
    back_w[LANES:, LANES:] = br.astype(BF16)

    for copy in copies_b:
        copy.wait_recv()
    quad[...] = dot(recv_b[...].reshape(FACETS * PATCH, PAIR), grid_w[...])
    grid_r = jnp.zeros((PATCH, SUBGRID), F32)
    grid_i = jnp.zeros((PATCH, SUBGRID), F32)
    for g in range(FACETS):
        rows = slice(PATCH * g, PATCH * (g + 1))
        qr, qi = quad[rows, 0:SUBGRID], quad[rows, SUBGRID:]
        pr, pi = ph_r[g : g + 1, :], ph_i[g : g + 1, :]
        grid_r += qr * pr - qi * pi
        grid_i += qr * pi + qi * pr
    grid_r = grid_r * (1.0 / CONTRIB)
    grid_i = grid_i * (1.0 / CONTRIB)

    patch_of = lax.shift_right_logical(iota((PATCH, SUBGRID), 1), 5)
    for c in range(SIDE):
        mine = patch_of == c
        gr = jnp.where(mine, grid_r, 0.0)
        gi = jnp.where(mine, grid_i, 0.0)
        rows = slice(PATCH * c, PATCH * (c + 1))
        low = slice(SUBGRID + PATCH * c, SUBGRID + PATCH * (c + 1))
        weigh[rows, 0:SUBGRID] = gr.astype(BF16)
        weigh[rows, SUBGRID:] = (-gi).astype(BF16)
        weigh[low, 0:SUBGRID] = gi.astype(BF16)
        weigh[low, SUBGRID:] = gr.astype(BF16)
    quad[...] = dot(weigh[...], ev[...])
    models_r, models_i = [], []
    for c in range(SIDE):
        rows = slice(PATCH * c, PATCH * (c + 1))
        low = slice(SUBGRID + PATCH * c, SUBGRID + PATCH * (c + 1))
        inner_r, inner_i = quad[rows, :], quad[low, :]
        ur, ui = eu_r[rows, :], eu_i[rows, :]
        models_r.append(jnp.sum(ur * inner_r - ui * inner_i, axis=0, keepdims=True))
        models_i.append(jnp.sum(ur * inner_i + ui * inner_r, axis=0, keepdims=True))
    model = jnp.concatenate(models_r + models_i, 0) * (1.0 / PATCH)
    residual = (seen_v[...].astype(F32) - model).astype(BF16)
    res_out[...] = residual
    residual = residual.astype(F32)
    for c in range(SIDE):
        rows = slice(PATCH * c, PATCH * (c + 1))
        low = slice(SUBGRID + PATCH * c, SUBGRID + PATCH * (c + 1))
        rr, ri = residual[c : c + 1, :], residual[SIDE + c : SIDE + c + 1, :]
        ur, ui = eu_r[rows, :], eu_i[rows, :]
        weigh[rows, :] = (rr * ur + ri * ui).astype(BF16)
        weigh[low, :] = (ri * ur - rr * ui).astype(BF16)
    quad[...] = lax.dot_general(
        weigh[...], ev[...], (((1,), (1,)), ((), ())), preferred_element_type=F32
    )
    back_r = jnp.zeros((PATCH, SUBGRID), F32)
    back_i = jnp.zeros((PATCH, SUBGRID), F32)
    for c in range(SIDE):
        mine = patch_of == c
        rows = slice(PATCH * c, PATCH * (c + 1))
        low = slice(SUBGRID + PATCH * c, SUBGRID + PATCH * (c + 1))
        back_r = jnp.where(mine, quad[rows, 0:SUBGRID] + quad[low, SUBGRID:], back_r)
        back_i = jnp.where(mine, quad[low, 0:SUBGRID] - quad[rows, SUBGRID:], back_i)
    back_r = back_r * (1.0 / math.sqrt(VIS))
    back_i = back_i * (1.0 / math.sqrt(VIS))

    for g in range(FACETS):
        rows = slice(PATCH * g, PATCH * (g + 1))
        pr, pi = ph_r[g : g + 1, :], ph_i[g : g + 1, :]
        shifted[rows, 0:SUBGRID] = (back_r * pr + back_i * pi).astype(BF16)
        shifted[rows, SUBGRID:] = (back_i * pr - back_r * pi).astype(BF16)
    narrowed = dot(shifted[...], narrow_w[...]).astype(BF16)
    send_c[...] = narrowed.reshape(FACETS, PATCH, PAIR)
    copies_c = exchange(2, "facet", f, facet_peers, lambda peer: send_c.at[peer], recv_c)
    recv_c[f] = send_c[f]

    for copy in copies_c:
        copy.wait_recv()
    came_back = recv_c[...].reshape(OWN, SUBGRID, PAIR)
    adjoint = []
    for j in range(OWN):
        both = dot(spread_h[...], came_back[j])
        ar = both[0:CONTRIB, 0:CONTRIB] - both[CONTRIB:, CONTRIB:]
        ai = both[0:CONTRIB, CONTRIB:] + both[CONTRIB:, 0:CONTRIB]
        adjoint.append((jnp.concatenate([ar, ai], 1) * (1.0 / SUBGRID)).astype(BF16))
    both = dot(row_h[...], jnp.concatenate(adjoint, 0))
    rr = both[0:FACET_ROWS, 0:CONTRIB] - both[FACET_ROWS:, CONTRIB:]
    ri = both[0:FACET_ROWS, CONTRIB:] + both[FACET_ROWS:, 0:CONTRIB]
    rows_sum = jnp.concatenate([rr, ri], 1).astype(BF16)
    send_d[...] = rows_sum.reshape(FREQS, ROWS_DEV, PAIR)
    copies_d = exchange(3, "freq", q, freq_peers, lambda peer: send_d.at[peer], recv_d)
    recv_d[q] = send_d[q]

    for copy in copies_d:
        copy.wait_recv()
    total = jnp.zeros((ROWS_DEV, PAIR), F32)
    for g in range(FREQS):
        total += recv_d[g].astype(F32)
    total = total * (1.0 / (math.sqrt(SUBGRIDS * CONTRIB) * math.sqrt(CONTRIB)))
    total_out[...] = total
    for copies in (copies_a, copies_b, copies_c, copies_d):
        for copy in copies:
            copy.wait_send()


def finish(total, tw_r, tw_i, back_w, residual, img_out, res_out, wide, image, out_sem):
    res_out[...] = residual[...]
    tot_r, tot_i = total[:, 0:CONTRIB], total[:, CONTRIB:]
    stores = []
    for part in range(PARTS):
        width = BLOCKS // PARTS
        for y in range(width * part, width * (part + 1)):
            rows = slice(ROWS_DEV * y, ROWS_DEV * (y + 1))
            cr, ci = tw_r[y : y + 1, :], tw_i[y : y + 1, :]
            wide[rows, 0:LANES] = (tot_r * cr - tot_i * ci).astype(BF16)
            wide[rows, LANES:] = (tot_r * ci + tot_i * cr).astype(BF16)
        rows = slice(ROWS_DEV * width * part, ROWS_DEV * width * (part + 1))
        prod = dot(wide[rows, :], back_w[...]).astype(BF16)
        for k in range(width):
            lanes = slice(LANES * (width * part + k), LANES * (width * part + k + 1))
            rows = slice(ROWS_DEV * k, ROWS_DEV * (k + 1))
            image[0:ROWS_DEV, lanes] = prod[rows, 0:LANES]
            image[ROWS_DEV:, lanes] = prod[rows, LANES:]
        lanes = pl.ds(LANES * width * part, LANES * width)
        store = pltpu.make_async_copy(image.at[:, lanes], img_out.at[:, lanes], out_sem.at[part])
        store.start()
        stores.append(store)
    for store in stores:
        store.wait()


def in_hbm(x):
    return pltpu.with_memory_space_constraint(x, pltpu.HBM)


def on_device(facet_image, facet_offsets, subgrid_rows, column_offset, uv_coords, observed):
    vmem = pl.BlockSpec(memory_space=pltpu.VMEM)
    smem = pl.BlockSpec(memory_space=pltpu.SMEM)
    hbm = pl.BlockSpec(memory_space=pltpu.HBM)
    chunk = pltpu.VMEM((16, 32, PAIR), BF16)
    *middle, residual = pl.pallas_call(
        kernel,
        out_shape=(
            jax.ShapeDtypeStruct((ROWS_DEV, PAIR), F32),
            jax.ShapeDtypeStruct((BLOCKS, LANES), F32),
            jax.ShapeDtypeStruct((BLOCKS, LANES), F32),
            jax.ShapeDtypeStruct((PAIR, PAIR), BF16),
            jax.ShapeDtypeStruct((2 * SIDE, VIS), BF16),
        ),
        in_specs=[hbm, hbm, smem, hbm, hbm, hbm],
        out_specs=(vmem,) * 5,
        scratch_shapes=[
            pltpu.SMEM((2, FACETS), jnp.int32),
            pltpu.SMEM((SUBGRIDS,), jnp.int32),
            pltpu.VMEM((2 * ROWS_DEV, FACET_W), BF16),
            pltpu.VMEM((2 * SIDE, VIS), jnp.int32),
            pltpu.VMEM((2 * SIDE, VIS), BF16),
            pltpu.VMEM((BLOCKS * ROWS_DEV, PAIR), BF16),
            pltpu.VMEM((BLOCKS * ROWS_DEV, PAIR), F32),
            pltpu.VMEM((PAIR, PAIR), BF16),
            pltpu.VMEM((2 * PAIR, FACET_ROWS), BF16),
            pltpu.VMEM((2 * FACET_ROWS, PAIR), BF16),
            pltpu.VMEM((2 * SUBGRID, CONTRIB), BF16),
            pltpu.VMEM((2 * CONTRIB, SUBGRID), BF16),
            pltpu.VMEM((PAIR, 2 * SUBGRID), BF16),
            pltpu.VMEM((2 * SUBGRID, PAIR), BF16),
            pltpu.VMEM((FACETS, SUBGRID), F32),
            pltpu.VMEM((FACETS, SUBGRID), F32),
            pltpu.VMEM((SUBGRID, VIS), F32),
            pltpu.VMEM((SUBGRID, VIS), F32),
            pltpu.VMEM((2 * SUBGRID, VIS), BF16),
            pltpu.VMEM((2 * SUBGRID, 2 * SUBGRID), F32),
            pltpu.VMEM((2 * SUBGRID, 2 * SUBGRID), BF16),
            pltpu.VMEM((2 * SUBGRID, 2 * SUBGRID), BF16),
            chunk,
            chunk,
            chunk,
            chunk,
            chunk,
            chunk,
            chunk,
            pltpu.SemaphoreType.DMA((6,)),
            pltpu.SemaphoreType.DMA((4, 15)),
            pltpu.SemaphoreType.DMA((4, 15)),
        ],
        compiler_params=pltpu.CompilerParams(
            collective_id=0, has_side_effects=True, vmem_limit_bytes=24 * 1024 * 1024
        ),
    )(
        in_hbm(facet_offsets.T),
        in_hbm(subgrid_rows),
        column_offset,
        in_hbm(facet_image.reshape(2 * ROWS_DEV, FACET_W)),
        in_hbm(uv_coords.reshape(2 * SIDE, VIS)),
        in_hbm(observed.reshape(2 * SIDE, VIS)),
    )
    image, residual = pl.pallas_call(
        finish,
        out_shape=(
            jax.ShapeDtypeStruct((2 * ROWS_DEV, FACET_W), BF16),
            jax.ShapeDtypeStruct((2 * SIDE, VIS), BF16),
        ),
        in_specs=[vmem] * 5,
        out_specs=(hbm, vmem),
        scratch_shapes=[
            pltpu.VMEM((BLOCKS * ROWS_DEV, PAIR), BF16),
            pltpu.VMEM((2 * ROWS_DEV, FACET_W), BF16),
            pltpu.SemaphoreType.DMA((PARTS,)),
        ],
        compiler_params=pltpu.CompilerParams(vmem_limit_bytes=24 * 1024 * 1024),
    )(*middle, residual)
    return (
        image.reshape(1, 2, ROWS_DEV, FACET_W),
        residual.reshape(2, 1, SIDE, VIS),
    )


def solution(mesh):
    return jax.shard_map(
        on_device,
        mesh=mesh,
        in_specs=(
            P("facet", None, "freq", None),
            P(),
            P(),
            P(),
            P(None, ("freq", "facet"), None, None),
            P(None, ("freq", "facet"), None, None),
        ),
        out_specs=(P("facet", None, "freq", None), P(None, ("freq", "facet"), None, None)),
        check_vma=False,
    )
```

```python
import math

import jax
import jax.numpy as jnp
from jax import lax
from jax.experimental import pallas as pl
from jax.experimental.pallas import tpu as pltpu
from jax.sharding import PartitionSpec as P

IMAGE = 32768
CONTRIB = 128
SUBGRID = 256
PATCH = 32
SIDE = 8
PERIOD = 256
COL_STEP = 8
ROW_STEP = 64
STEP = 128
FACETS = 16
FREQS = 16
ROWS_DEV = 32
FACET_ROWS = FREQS * ROWS_DEV
FACET_W = 4096
SUBGRIDS = 32
OWN = 2
VIS = 512
LANES = 128
BLOCKS = FACET_W // LANES
PAIR = 2 * CONTRIB
PARTS = 4
HALF = FACET_ROWS // 2
FAR_Z = (2, 1, 3, 0)

TWO_PI = 2.0 * math.pi
MESH = pl.DeviceIdType.MESH
F32 = jnp.float32
BF16 = jnp.bfloat16


def ring_hops(step, size):
    return min(step, size - step)


FACET_STEPS = sorted(
    [(x, z) for x in range(4) for z in range(4) if x or z],
    key=lambda s: -ring_hops(s[0], 4) - 2 * ring_hops(s[1], 4),
)
FREQ_STEPS = sorted(
    [(z, y, c) for z in range(2) for y in range(4) for c in range(2) if z or y or c],
    key=lambda s: -s[0] - ring_hops(s[1], 4),
)


def facet_peer(f, step):
    return lax.rem(f // 4 + step[0], 4) * 4 + lax.rem(lax.rem(f, 4) + step[1], 4)


def freq_peer(q, step):
    z, y, c = q // 8, lax.rem(q // 2, 4), lax.rem(q, 2)
    return (lax.rem(z + step[0], 2) * 4 + lax.rem(y + step[1], 4)) * 2 + lax.rem(c + step[2], 2)


def iota(shape, dim):
    return lax.broadcasted_iota(jnp.int32, shape, dim)


def wrap(m):
    return m & (IMAGE - 1)


def cis(m, period=IMAGE):
    quarter = period // 4
    m = m & (period - 1)
    turn = lax.shift_right_logical(m + quarter // 2, int(math.log2(quarter)))
    rest = (m - turn * quarter).astype(F32) * (TWO_PI / period)
    sq = rest * rest
    sin = 1.0 / 120.0 + sq * (-1.0 / 5040.0 + sq * (1.0 / 362880.0))
    sin = rest + rest * (sq * (-1.0 / 6.0 + sq * sin))
    cos = 1.0 / 24.0 + sq * (-1.0 / 720.0 + sq * (1.0 / 40320.0))
    cos = 1.0 + sq * (-0.5 + sq * cos)
    odd = (turn & 1) == 1
    c = jnp.where(odd, sin, cos)
    s = jnp.where(odd, cos, sin)
    c = jnp.where(((turn + 1) & 2) == 2, -c, c)
    s = jnp.where((turn & 2) == 2, -s, s)
    return c, s


def cmul(a, b):
    return a[0] * b[0] - a[1] * b[1], a[0] * b[1] + a[1] * b[0]


def outer(fine, coarse):
    rows = [
        cmul(fine, (coarse[0][h : h + 1], coarse[1][h : h + 1])) for h in range(coarse[0].shape[0])
    ]
    return jnp.concatenate([r[0] for r in rows], 0), jnp.concatenate([r[1] for r in rows], 0)


def dot(a, b):
    return jnp.dot(a, b, preferred_element_type=F32)


def kernel(
    offs_in,
    starts_in,
    col_s,
    facet_in,
    uv_in,
    seen_in,
    total_out,
    tw_r,
    tw_i,
    back_w,
    res_out,
    offs_s,
    starts_s,
    facet_v,
    uv_v,
    seen_v,
    wide,
    col_w,
    row_t,
    row_h,
    spread_t,
    spread_h,
    grid_w,
    narrow_w,
    ph_r,
    ph_i,
    eu_r,
    eu_i,
    ev,
    quad,
    cells,
    weigh,
    shifted,
    gath,
    send_b,
    recv_b,
    send_c,
    recv_c,
    send_d,
    recv_d,
    in_sem,
    load_sem,
    tx_sem,
    rx_sem,
):
    f = lax.axis_index("facet")
    q = lax.axis_index("freq")

    loads = [
        pltpu.make_async_copy(src, dst, in_sem.at[3 + i])
        for i, (src, dst) in enumerate(
            ((offs_in, offs_s), (starts_in, starts_s))
        )
    ]
    for copy in loads:
        copy.start()
    load = []
    for i in range(PARTS):
        lanes = pl.ds(FACET_W // PARTS * i, FACET_W // PARTS)
        load.append(
            pltpu.make_async_copy(
                facet_in.at[:, lanes], facet_v.at[:, lanes], load_sem.at[i]
            )
        )
        load[i].start()
    load_uv = pltpu.make_async_copy(uv_in, uv_v, in_sem.at[1])
    load_uv.start()
    load_seen = pltpu.make_async_copy(seen_in, seen_v, in_sem.at[2])
    load_seen.start()

    barrier = pltpu.get_barrier_semaphore()
    facet_peers = [facet_peer(f, step) for step in FACET_STEPS]
    freq_peers = [freq_peer(q, step) for step in FREQ_STEPS]
    for peer in facet_peers:
        pl.semaphore_signal(barrier, inc=1, device_id={"facet": peer}, device_id_type=MESH)
    for peer in freq_peers:
        pl.semaphore_signal(barrier, inc=1, device_id={"freq": peer}, device_id_type=MESH)

    for copy in loads:
        copy.wait()
    a = offs_s[0, f]
    b = offs_s[1, f]
    column = col_s[0]
    start0 = starts_s[OWN * q]
    start1 = starts_s[OWN * q + 1]

    def facet_group(dz):
        return [(i, p) for i, p in enumerate(facet_peers) if FACET_STEPS[i][1] == dz]

    def freq_group(dz):
        return [(i, p) for i, p in enumerate(freq_peers) if FREQ_STEPS[i][0] == dz]

    def exchange(stage, axis, me, peers, src, dst):
        copies = []
        for i, peer in peers:
            copies.append(
                pltpu.make_async_remote_copy(
                    src_ref=src(peer),
                    dst_ref=dst.at[me],
                    send_sem=tx_sem.at[stage, i],
                    recv_sem=rx_sem.at[stage, i],
                    device_id={axis: peer},
                    device_id_type=MESH,
                )
            )
        for copy in copies:
            copy.start()
        return copies

    freq_l = wrap(column + COL_STEP * iota((8, LANES), 1))
    fine = cis(freq_l * iota((8, LANES), 0))
    freq_h = wrap(column + COL_STEP * iota((16, LANES), 1))
    coarse = cis(freq_h * (8 * iota((16, LANES), 0)))
    tr, ti = outer(fine, coarse)
    ti = -ti
    col_w[0:LANES, 0:LANES] = tr.astype(BF16)
    col_w[0:LANES, LANES:] = ti.astype(BF16)
    col_w[LANES:, 0:LANES] = (-ti).astype(BF16)
    col_w[LANES:, LANES:] = tr.astype(BF16)
    freq_b = wrap(column + COL_STEP * iota((BLOCKS, LANES), 1))
    wr, wi = cis(freq_b * wrap(b + LANES * iota((BLOCKS, LANES), 0)))
    tw_r[...] = wr
    tw_i[...] = wi

    acc_r = jnp.zeros((ROWS_DEV, LANES), F32)
    acc_i = jnp.zeros((ROWS_DEV, LANES), F32)
    width = BLOCKS // PARTS
    for part in range(PARTS):
        load[part].wait()
        for y in range(width * part, width * (part + 1)):
            rows = slice(ROWS_DEV * y, ROWS_DEV * (y + 1))
            lanes = slice(LANES * y, LANES * (y + 1))
            wide[rows, 0:LANES] = facet_v[0:ROWS_DEV, lanes]
            wide[rows, LANES:] = facet_v[ROWS_DEV:, lanes]
        rows = slice(ROWS_DEV * width * part, ROWS_DEV * width * (part + 1))
        prod = dot(wide[rows, :], col_w[...])
        for k in range(width):
            y = width * part + k
            rows = slice(ROWS_DEV * k, ROWS_DEV * (k + 1))
            dr, di = prod[rows, 0:LANES], prod[rows, LANES:]
            cr, ci = tw_r[y : y + 1, :], tw_i[y : y + 1, :]
            acc_r += dr * cr + di * ci
            acc_i += di * cr - dr * ci
    transformed = jnp.concatenate([acc_r, acc_i], 1) * (1.0 / math.sqrt(FACET_W))
    gath[q] = transformed.astype(BF16)

    pl.semaphore_wait(barrier, FACETS - 1 + FREQS - 1)
    copies_a = exchange(0, "freq", q, list(enumerate(freq_peers)), lambda peer: gath.at[q], gath)

    place = wrap(a + iota((8, FACET_ROWS), 1))
    coarse = cis(8 * ROW_STEP * iota((16, FACET_ROWS), 0) * wrap(a + iota((16, FACET_ROWS), 1)))
    for j, start in enumerate((start0, start1)):
        fine = cis(wrap(start + ROW_STEP * iota((8, FACET_ROWS), 0)) * place)
        rr, ri = outer(fine, coarse)
        for z in range(2):
            lanes = slice(HALF * z, HALF * (z + 1))
            row_t[z, CONTRIB * j : CONTRIB * (j + 1), :] = rr[:, lanes].astype(BF16)
            low = slice(PAIR + CONTRIB * j, PAIR + CONTRIB * (j + 1))
            row_t[z, low, :] = (-ri[:, lanes]).astype(BF16)

    lane_k = iota((8, CONTRIB), 1)
    fine = cis(iota((8, CONTRIB), 0) * wrap(STEP * lane_k + a))
    coarse = cis(8 * iota((32, CONTRIB), 0) * wrap(STEP * iota((32, CONTRIB), 1) + a))
    sr, si = outer(fine, coarse)
    for g in range(SIDE):
        rows = slice(PATCH * g, PATCH * (g + 1))
        half = PATCH * (g // 4)
        spread_t[g % 4, half : half + PATCH, :] = sr[rows].astype(BF16)
        spread_t[g % 4, 2 * PATCH + half : 3 * PATCH + half, :] = si[rows].astype(BF16)

    fine = cis(STEP * iota((8, SUBGRID), 0) * iota((8, SUBGRID), 1))
    coarse = cis(8 * STEP * iota((16, SUBGRID), 0) * iota((16, SUBGRID), 1))
    gr, gi = outer(fine, coarse)
    grid_w[0:CONTRIB, 0:SUBGRID] = gr.astype(BF16)
    grid_w[0:CONTRIB, SUBGRID:] = gi.astype(BF16)
    grid_w[CONTRIB:, 0:SUBGRID] = (-gi).astype(BF16)
    grid_w[CONTRIB:, SUBGRID:] = gr.astype(BF16)

    shift_b = jnp.concatenate(
        [jnp.full((1, SUBGRID), offs_s[1, g], jnp.int32) for g in range(FACETS)], 0
    )
    pr, pi = cis(iota((FACETS, SUBGRID), 1) * shift_b)
    ph_r[...] = pr
    ph_i[...] = pi

    def own_half(z):
        return dot(row_t[z], gath[pl.ds(8 * z, 8)].reshape(HALF, PAIR))

    for copy, step in zip(copies_a, FREQ_STEPS):
        if step[0] == 0:
            copy.wait_recv()
    both = own_half(q // 8)
    for copy, step in zip(copies_a, FREQ_STEPS):
        if step[0] == 1:
            copy.wait_recv()
    both += own_half(1 - q // 8)
    cr = both[0:PAIR, 0:CONTRIB] - both[PAIR:, CONTRIB:]
    ci = both[0:PAIR, CONTRIB:] + both[PAIR:, 0:CONTRIB]
    contrib = (jnp.concatenate([cr, ci], 1) * (1.0 / math.sqrt(FACET_ROWS))).astype(BF16)
    contrib = jnp.concatenate([contrib[CONTRIB * j : CONTRIB * (j + 1)] for j in range(OWN)], 1)
    copies_b = []
    for dz in FAR_Z:
        z = lax.rem(lax.rem(f, 4) + dz, 4)
        both = dot(spread_t[z], contrib)
        for j in range(OWN):
            re, im = slice(PAIR * j, PAIR * j + CONTRIB), slice(PAIR * j + CONTRIB, PAIR * (j + 1))
            sr = both[0 : 2 * PATCH, re] - both[2 * PATCH :, im]
            si = both[0 : 2 * PATCH, im] + both[2 * PATCH :, re]
            part = jnp.concatenate([sr, si], 1).astype(BF16)
            send_b[8 * j + z] = part[0:PATCH]
            send_b[8 * j + 4 + z] = part[PATCH:]
        copies_b += exchange(1, "facet", f, facet_group(dz), lambda peer: send_b.at[peer], recv_b)
    recv_b[f] = send_b[f]

    load_uv.wait()
    load_seen.wait()

    def patch_rows(coords):
        cell = iota((8, VIS), 0)
        by8 = cis(8 * coords, PERIOD)
        by16 = cis(16 * coords, PERIOD)
        for c in range(SIDE):
            row = jnp.broadcast_to(coords[c : c + 1], (8, VIS))
            low = cis(cell * row, PERIOD)
            mid = cmul(low, (by8[0][c : c + 1], by8[1][c : c + 1]))
            half = (jnp.concatenate([low[0], mid[0]], 0), jnp.concatenate([low[1], mid[1]], 0))
            high = cmul(half, (by16[0][c : c + 1], by16[1][c : c + 1]))
            yield (
                c,
                jnp.concatenate([half[0], high[0]], 0),
                jnp.concatenate([half[1], high[1]], 0),
            )

    for c, er, ei in patch_rows(uv_v[0:SIDE, :]):
        eu_r[PATCH * c : PATCH * (c + 1), :] = er
        eu_i[PATCH * c : PATCH * (c + 1), :] = ei
    for c, er, ei in patch_rows(uv_v[SIDE:, :]):
        first = PATCH * (c % 4)
        ev[c // 4, first : first + PATCH, :] = er.astype(BF16)
        ev[c // 4, LANES + first : LANES + first + PATCH, :] = ei.astype(BF16)

    fine = cis(STEP * iota((8, CONTRIB), 0) * lane_k)
    coarse = cis(8 * STEP * iota((32, CONTRIB), 0) * iota((32, CONTRIB), 1))
    nr, ni = outer(fine, coarse)
    narrow_w[0:SUBGRID, 0:CONTRIB] = nr.astype(BF16)
    narrow_w[0:SUBGRID, CONTRIB:] = (-ni).astype(BF16)
    narrow_w[SUBGRID:, 0:CONTRIB] = ni.astype(BF16)
    narrow_w[SUBGRID:, CONTRIB:] = nr.astype(BF16)

    fine = cis(wrap(STEP * iota((8, SUBGRID), 0) + a) * iota((8, SUBGRID), 1))
    coarse = cis(8 * STEP * iota((16, SUBGRID), 0) * iota((16, SUBGRID), 1))
    hr, hi = outer(fine, coarse)
    spread_h[0:CONTRIB, :] = hr.astype(BF16)
    spread_h[CONTRIB:, :] = (-hi).astype(BF16)

    def own_freq(rows):
        lane = iota((rows, PAIR), 1)
        start = jnp.where(lane < CONTRIB, start0, start1)
        return wrap(start + ROW_STEP * (lane & (CONTRIB - 1)))

    fine = cis(own_freq(8) * wrap(a + iota((8, PAIR), 0)))
    coarse = cis(own_freq(FACET_ROWS // 8) * (8 * iota((FACET_ROWS // 8, PAIR), 0)))
    hr, hi = outer(fine, coarse)
    for z in range(2):
        rows = slice(HALF * z, HALF * (z + 1))
        row_h[z, 0:HALF, :] = hr[rows].astype(BF16)
        row_h[z, HALF:, :] = hi[rows].astype(BF16)

    fine = cis(wrap(column + COL_STEP * iota((8, LANES), 0)) * iota((8, LANES), 1))
    coarse = cis(8 * COL_STEP * iota((16, LANES), 0) * iota((16, LANES), 1))
    br, bi = outer(fine, coarse)
    back_w[0:LANES, 0:LANES] = br.astype(BF16)
    back_w[0:LANES, LANES:] = bi.astype(BF16)
    back_w[LANES:, 0:LANES] = (-bi).astype(BF16)
    back_w[LANES:, LANES:] = br.astype(BF16)

    grid_r = jnp.zeros((PATCH, SUBGRID), F32)
    grid_i = jnp.zeros((PATCH, SUBGRID), F32)
    order_b = [FACET_STEPS[i] for dz in FAR_Z for i, _ in facet_group(dz)]
    for dz in FAR_Z[::-1]:
        for copy, step in zip(copies_b, order_b):
            if step[1] == (4 - dz) % 4:
                copy.wait_recv()
        senders = [4 * x + lax.rem(lax.rem(f, 4) + dz, 4) for x in range(4)]
        rows = jnp.concatenate([recv_b[g] for g in senders], 0)
        part = dot(rows, grid_w[...])
        for x, g in enumerate(senders):
            rows = slice(PATCH * x, PATCH * (x + 1))
            qr, qi = part[rows, 0:SUBGRID], part[rows, SUBGRID:]
            pr, pi = ph_r[pl.ds(g, 1), :], ph_i[pl.ds(g, 1), :]
            grid_r += qr * pr - qi * pi
            grid_i += qr * pi + qi * pr
    grid_r = grid_r * (1.0 / CONTRIB)
    grid_i = grid_i * (1.0 / CONTRIB)

    patch_of = lax.shift_right_logical(iota((PATCH, LANES), 1), 5)
    for c in range(SIDE):
        mine = patch_of == c % 4
        lanes = slice(LANES * (c // 4), LANES * (c // 4 + 1))
        gr = jnp.where(mine, grid_r[:, lanes], 0.0)
        gi = jnp.where(mine, grid_i[:, lanes], 0.0)
        first = PATCH * (c % 4)
        rows = slice(first, first + PATCH)
        low = slice(LANES + first, LANES + first + PATCH)
        cells[c // 4, rows, 0:LANES] = gr.astype(BF16)
        cells[c // 4, rows, LANES:] = (-gi).astype(BF16)
        cells[c // 4, low, 0:LANES] = gi.astype(BF16)
        cells[c // 4, low, LANES:] = gr.astype(BF16)
    models_r, models_i = [], []
    for h in range(2):
        quad[h] = dot(cells[h], ev[h])
    for c in range(SIDE):
        first = PATCH * (c % 4)
        inner_r = quad[c // 4, first : first + PATCH, :]
        inner_i = quad[c // 4, LANES + first : LANES + first + PATCH, :]
        ur, ui = eu_r[PATCH * c : PATCH * (c + 1), :], eu_i[PATCH * c : PATCH * (c + 1), :]
        models_r.append(jnp.sum(ur * inner_r - ui * inner_i, axis=0, keepdims=True))
        models_i.append(jnp.sum(ur * inner_i + ui * inner_r, axis=0, keepdims=True))
    model = jnp.concatenate(models_r + models_i, 0) * (1.0 / PATCH)
    residual = (seen_v[...].astype(F32) - model).astype(BF16)
    res_out[...] = residual
    residual = residual.astype(F32)
    backs_r, backs_i = [], []
    for h in range(2):
        for c in range(4 * h, 4 * (h + 1)):
            first = PATCH * (c % 4)
            rr, ri = residual[c : c + 1, :], residual[SIDE + c : SIDE + c + 1, :]
            ur, ui = eu_r[PATCH * c : PATCH * (c + 1), :], eu_i[PATCH * c : PATCH * (c + 1), :]
            weigh[h, first : first + PATCH, :] = (rr * ur + ri * ui).astype(BF16)
            weigh[h, LANES + first : LANES + first + PATCH, :] = (ri * ur - rr * ui).astype(BF16)
        full = lax.dot_general(
            weigh[h], ev[h], (((1,), (1,)), ((), ())), preferred_element_type=F32
        )
        back_r = jnp.zeros((PATCH, LANES), F32)
        back_i = jnp.zeros((PATCH, LANES), F32)
        for c in range(4):
            mine = patch_of == c
            rows = slice(PATCH * c, PATCH * (c + 1))
            low = slice(LANES + PATCH * c, LANES + PATCH * (c + 1))
            back_r = jnp.where(mine, full[rows, 0:LANES] + full[low, LANES:], back_r)
            back_i = jnp.where(mine, full[low, 0:LANES] - full[rows, LANES:], back_i)
        backs_r.append(back_r)
        backs_i.append(back_i)
    back_r = jnp.concatenate(backs_r, 1)
    back_i = jnp.concatenate(backs_i, 1)
    back_r = back_r * (1.0 / math.sqrt(VIS))
    back_i = back_i * (1.0 / math.sqrt(VIS))

    copies_c = []
    for n, dz in enumerate(FAR_Z):
        takers = [4 * x + lax.rem(lax.rem(f, 4) + dz, 4) for x in range(4)]
        for x, g in enumerate(takers):
            rows = slice(PATCH * x, PATCH * (x + 1))
            pr, pi = ph_r[pl.ds(g, 1), :], ph_i[pl.ds(g, 1), :]
            shifted[n, rows, 0:SUBGRID] = (back_r * pr + back_i * pi).astype(BF16)
            shifted[n, rows, SUBGRID:] = (back_i * pr - back_r * pi).astype(BF16)
        narrowed = dot(shifted[n], narrow_w[...]).astype(BF16)
        for x, g in enumerate(takers):
            send_c[g] = narrowed[PATCH * x : PATCH * (x + 1)]
        copies_c += exchange(2, "facet", f, facet_group(dz), lambda peer: send_c.at[peer], recv_c)
    recv_c[f] = send_c[f]

    for copy in copies_c:
        copy.wait_recv()
    came_back = recv_c[...].reshape(OWN, SUBGRID, PAIR)
    adjoint = []
    for j in range(OWN):
        both = dot(spread_h[...], came_back[j])
        ar = both[0:CONTRIB, 0:CONTRIB] - both[CONTRIB:, CONTRIB:]
        ai = both[0:CONTRIB, CONTRIB:] + both[CONTRIB:, 0:CONTRIB]
        adjoint.append((jnp.concatenate([ar, ai], 1) * (1.0 / SUBGRID)).astype(BF16))
    adjoint = jnp.concatenate(adjoint, 0)
    copies_d = []
    for dz in (1, 0):
        z = lax.rem(q // 8 + dz, 2)
        both = dot(row_h[z], adjoint)
        rr = both[0:HALF, 0:CONTRIB] - both[HALF:, CONTRIB:]
        ri = both[0:HALF, CONTRIB:] + both[HALF:, 0:CONTRIB]
        rows = jnp.concatenate([rr, ri], 1).astype(BF16)
        send_d[pl.ds(8 * z, 8)] = rows.reshape(8, ROWS_DEV, PAIR)
        copies_d += exchange(3, "freq", q, freq_group(dz), lambda peer: send_d.at[peer], recv_d)

    total = send_d[q].astype(F32)
    order_d = [FREQ_STEPS[i] for dz in (1, 0) for i, _ in freq_group(dz)]
    for copy, step in list(zip(copies_d, order_d))[::-1]:
        copy.wait_recv()
        total += recv_d[freq_peer(q, (-step[0] % 2, -step[1] % 4, -step[2] % 2))].astype(F32)
    total = total * (1.0 / (math.sqrt(SUBGRIDS * CONTRIB) * math.sqrt(CONTRIB)))
    total_out[...] = total
    for copies in (copies_a, copies_b, copies_c, copies_d):
        for copy in copies:
            copy.wait_send()


def finish(total, tw_r, tw_i, back_w, residual, img_out, res_out, wide, image, out_sem):
    stores = [pltpu.make_async_copy(residual, res_out, out_sem.at[PARTS])]
    stores[0].start()
    tot_r, tot_i = total[:, 0:CONTRIB], total[:, CONTRIB:]
    for part in range(PARTS):
        width = BLOCKS // PARTS
        for y in range(width * part, width * (part + 1)):
            rows = slice(ROWS_DEV * y, ROWS_DEV * (y + 1))
            cr, ci = tw_r[y : y + 1, :], tw_i[y : y + 1, :]
            wide[rows, 0:LANES] = (tot_r * cr - tot_i * ci).astype(BF16)
            wide[rows, LANES:] = (tot_r * ci + tot_i * cr).astype(BF16)
        rows = slice(ROWS_DEV * width * part, ROWS_DEV * width * (part + 1))
        prod = dot(wide[rows, :], back_w[...]).astype(BF16)
        for k in range(width):
            lanes = slice(LANES * (width * part + k), LANES * (width * part + k + 1))
            rows = slice(ROWS_DEV * k, ROWS_DEV * (k + 1))
            image[0:ROWS_DEV, lanes] = prod[rows, 0:LANES]
            image[ROWS_DEV:, lanes] = prod[rows, LANES:]
        lanes = pl.ds(LANES * width * part, LANES * width)
        store = pltpu.make_async_copy(image.at[:, lanes], img_out.at[:, lanes], out_sem.at[part])
        store.start()
        stores.append(store)
    for store in stores:
        store.wait()


def in_hbm(x):
    return pltpu.with_memory_space_constraint(x, pltpu.HBM)


def on_device(facet_image, facet_offsets, subgrid_rows, column_offset, uv_coords, observed):
    vmem = pl.BlockSpec(memory_space=pltpu.VMEM)
    smem = pl.BlockSpec(memory_space=pltpu.SMEM)
    hbm = pl.BlockSpec(memory_space=pltpu.HBM)
    chunk = pltpu.VMEM((16, 32, PAIR), BF16)
    *middle, residual = pl.pallas_call(
        kernel,
        out_shape=(
            jax.ShapeDtypeStruct((ROWS_DEV, PAIR), F32),
            jax.ShapeDtypeStruct((BLOCKS, LANES), F32),
            jax.ShapeDtypeStruct((BLOCKS, LANES), F32),
            jax.ShapeDtypeStruct((PAIR, PAIR), BF16),
            jax.ShapeDtypeStruct((2 * SIDE, VIS), BF16),
        ),
        in_specs=[hbm, hbm, smem, hbm, hbm, hbm],
        out_specs=(vmem,) * 5,
        scratch_shapes=[
            pltpu.SMEM((2, FACETS), jnp.int32),
            pltpu.SMEM((SUBGRIDS,), jnp.int32),
            pltpu.VMEM((2 * ROWS_DEV, FACET_W), BF16),
            pltpu.VMEM((2 * SIDE, VIS), jnp.int32),
            pltpu.VMEM((2 * SIDE, VIS), BF16),
            pltpu.VMEM((BLOCKS * ROWS_DEV, PAIR), BF16),
            pltpu.VMEM((PAIR, PAIR), BF16),
            pltpu.VMEM((2, 2 * PAIR, HALF), BF16),
            pltpu.VMEM((2, 2 * HALF, PAIR), BF16),
            pltpu.VMEM((4, 4 * PATCH, CONTRIB), BF16),
            pltpu.VMEM((2 * CONTRIB, SUBGRID), BF16),
            pltpu.VMEM((PAIR, 2 * SUBGRID), BF16),
            pltpu.VMEM((2 * SUBGRID, PAIR), BF16),
            pltpu.VMEM((FACETS, SUBGRID), F32),
            pltpu.VMEM((FACETS, SUBGRID), F32),
            pltpu.VMEM((SUBGRID, VIS), F32),
            pltpu.VMEM((SUBGRID, VIS), F32),
            pltpu.VMEM((2, SUBGRID, VIS), BF16),
            pltpu.VMEM((2, SUBGRID, VIS), F32),
            pltpu.VMEM((2, SUBGRID, SUBGRID), BF16),
            pltpu.VMEM((2, SUBGRID, VIS), BF16),
            pltpu.VMEM((4, 4 * PATCH, 2 * SUBGRID), BF16),
            chunk,
            chunk,
            chunk,
            chunk,
            chunk,
            chunk,
            chunk,
            pltpu.SemaphoreType.DMA((6,)),
            pltpu.SemaphoreType.DMA((PARTS,)),
            pltpu.SemaphoreType.DMA((4, 15)),
            pltpu.SemaphoreType.DMA((4, 15)),
        ],
        compiler_params=pltpu.CompilerParams(
            collective_id=0, has_side_effects=True, vmem_limit_bytes=24 * 1024 * 1024
        ),
    )(
        in_hbm(facet_offsets.T),
        in_hbm(subgrid_rows),
        column_offset,
        in_hbm(facet_image.reshape(2 * ROWS_DEV, FACET_W)),
        in_hbm(uv_coords.reshape(2 * SIDE, VIS)),
        in_hbm(observed.reshape(2 * SIDE, VIS)),
    )
    image, residual = pl.pallas_call(
        finish,
        out_shape=(
            jax.ShapeDtypeStruct((2 * ROWS_DEV, FACET_W), BF16),
            jax.ShapeDtypeStruct((2 * SIDE, VIS), BF16),
        ),
        in_specs=[vmem] * 5,
        out_specs=(hbm, hbm),
        scratch_shapes=[
            pltpu.VMEM((BLOCKS * ROWS_DEV, PAIR), BF16),
            pltpu.VMEM((2 * ROWS_DEV, FACET_W), BF16),
            pltpu.SemaphoreType.DMA((PARTS + 1,)),
        ],
        compiler_params=pltpu.CompilerParams(vmem_limit_bytes=24 * 1024 * 1024),
    )(*middle, residual)
    return (
        image.reshape(1, 2, ROWS_DEV, FACET_W),
        residual.reshape(2, 1, SIDE, VIS),
    )


def solution(mesh):
    return jax.shard_map(
        on_device,
        mesh=mesh,
        in_specs=(
            P("facet", None, "freq", None),
            P(),
            P(),
            P(),
            P(None, ("freq", "facet"), None, None),
            P(None, ("freq", "facet"), None, None),
        ),
        out_specs=(P("facet", None, "freq", None), P(None, ("freq", "facet"), None, None)),
        check_vma=False,
    )
```

```python
import math

import jax
import jax.numpy as jnp
from jax import lax
from jax.experimental import pallas as pl
from jax.experimental.pallas import tpu as pltpu
from jax.sharding import PartitionSpec as P

IMAGE = 32768
CONTRIB = 128
SUBGRID = 256
PATCH = 32
SIDE = 8
PERIOD = 256
COL_STEP = 8
ROW_STEP = 64
STEP = 128
FACETS = 16
FREQS = 16
ROWS_DEV = 32
FACET_ROWS = FREQS * ROWS_DEV
FACET_W = 4096
SUBGRIDS = 32
OWN = 2
VIS = 512
LANES = 128
BLOCKS = FACET_W // LANES
PAIR = 2 * CONTRIB
PARTS = 4
HALF = FACET_ROWS // 2

TWO_PI = 2.0 * math.pi
MESH = pl.DeviceIdType.MESH
F32 = jnp.float32
BF16 = jnp.bfloat16


def ring_hops(step, size):
    return min(step, size - step)


SPREAD_STEPS = [(x, d) for d in (3, 2, 1, 0) for x in (2, 1, 3, 0) if x or d]
FREQ_STEPS = sorted(
    [(z, y, c) for z in range(2) for y in range(4) for c in range(2) if z or y or c],
    key=lambda s: -s[0] - ring_hops(s[1], 4),
)


def freq_peer(q, step):
    z, y, c = q // 8, lax.rem(q // 2, 4), lax.rem(q, 2)
    return (lax.rem(z + step[0], 2) * 4 + lax.rem(y + step[1], 4)) * 2 + lax.rem(c + step[2], 2)


def back_step(d):
    return d if d % 2 else -d


def iota(shape, dim):
    return lax.broadcasted_iota(jnp.int32, shape, dim)


def wrap(m):
    return m & (IMAGE - 1)


def cis(m, period=IMAGE):
    quarter = period // 4
    m = m & (period - 1)
    turn = lax.shift_right_logical(m + quarter // 2, int(math.log2(quarter)))
    rest = (m - turn * quarter).astype(F32) * (TWO_PI / period)
    sq = rest * rest
    sin = 1.0 / 120.0 + sq * (-1.0 / 5040.0 + sq * (1.0 / 362880.0))
    sin = rest + rest * (sq * (-1.0 / 6.0 + sq * sin))
    cos = 1.0 / 24.0 + sq * (-1.0 / 720.0 + sq * (1.0 / 40320.0))
    cos = 1.0 + sq * (-0.5 + sq * cos)
    odd = (turn & 1) == 1
    c = jnp.where(odd, sin, cos)
    s = jnp.where(odd, cos, sin)
    c = jnp.where(((turn + 1) & 2) == 2, -c, c)
    s = jnp.where((turn & 2) == 2, -s, s)
    return c, s


def cmul(a, b):
    return a[0] * b[0] - a[1] * b[1], a[0] * b[1] + a[1] * b[0]


def outer(fine, coarse):
    rows = [
        cmul(fine, (coarse[0][h : h + 1], coarse[1][h : h + 1])) for h in range(coarse[0].shape[0])
    ]
    return jnp.concatenate([r[0] for r in rows], 0), jnp.concatenate([r[1] for r in rows], 0)


def dot(a, b):
    return jnp.dot(a, b, preferred_element_type=F32)


def kernel(
    offs_in,
    starts_in,
    col_s,
    facet_in,
    uv_in,
    seen_in,
    total_out,
    tw_r,
    tw_i,
    back_w,
    res_out,
    offs_s,
    starts_s,
    facet_v,
    uv_v,
    seen_v,
    wide,
    col_w,
    row_t,
    row_h,
    spread_t,
    spread_h,
    grid_w,
    narrow_w,
    ph_r,
    ph_i,
    eu_r,
    eu_i,
    ev,
    quad,
    cells,
    weigh,
    shifted,
    gath,
    send_b,
    recv_b,
    send_c,
    recv_c,
    send_d,
    recv_d,
    in_sem,
    load_sem,
    tx_sem,
    rx_sem,
):
    f = lax.axis_index("facet")
    q = lax.axis_index("freq")

    loads = [
        pltpu.make_async_copy(src, dst, in_sem.at[3 + i])
        for i, (src, dst) in enumerate(
            ((offs_in, offs_s), (starts_in, starts_s))
        )
    ]
    for copy in loads:
        copy.start()
    load = []
    for i in range(PARTS):
        lanes = pl.ds(FACET_W // PARTS * i, FACET_W // PARTS)
        load.append(
            pltpu.make_async_copy(
                facet_in.at[:, lanes], facet_v.at[:, lanes], load_sem.at[i]
            )
        )
        load[i].start()
    load_uv = pltpu.make_async_copy(uv_in, uv_v, in_sem.at[1])
    load_uv.start()
    load_seen = pltpu.make_async_copy(seen_in, seen_v, in_sem.at[2])
    load_seen.start()

    barrier = pltpu.get_barrier_semaphore()
    x, chip, other = f // 4, 2 * lax.rem(f, 4) + q // 8, lax.rem(q + 8, FREQS)
    away = 2 * (q // 8) - 1

    def beside(dx, dz):
        z = lax.rem(chip + away * dz + 8, 8)
        return {"facet": 4 * lax.rem(x + dx, 4) + z // 2, "freq": other if dz % 2 else q}

    def target(d):
        return lax.rem(chip + away * d + 8, 8) // 2

    def origin(d):
        return lax.rem(chip + away * back_step(d) + 8, 8) // 2

    freq_peers = [freq_peer(q, step) for step in FREQ_STEPS]
    greeted = [(dx, dz) for dx in range(4) for dz in (0, 1, 2, 3, -2) if dx or dz]
    for dx, dz in greeted:
        pl.semaphore_signal(barrier, inc=1, device_id=beside(dx, dz), device_id_type=MESH)
    for peer in freq_peers:
        pl.semaphore_signal(barrier, inc=1, device_id={"freq": peer}, device_id_type=MESH)

    for copy in loads:
        copy.wait()
    a = offs_s[0, f]
    b = offs_s[1, f]
    column = col_s[0]
    starts = [starts_s[OWN * who + j] for who in (q, other) for j in range(OWN)]

    def freq_group(dz):
        return [(i, p) for i, p in enumerate(freq_peers) if FREQ_STEPS[i][0] == dz]

    def send(stage, i, src, dst, device):
        copy = pltpu.make_async_remote_copy(
            src_ref=src,
            dst_ref=dst,
            send_sem=tx_sem.at[stage, i],
            recv_sem=rx_sem.at[stage, i],
            device_id=device,
            device_id_type=MESH,
        )
        copy.start()
        return copy

    freq_l = wrap(column + COL_STEP * iota((8, LANES), 1))
    fine = cis(freq_l * iota((8, LANES), 0))
    freq_h = wrap(column + COL_STEP * iota((16, LANES), 1))
    coarse = cis(freq_h * (8 * iota((16, LANES), 0)))
    tr, ti = outer(fine, coarse)
    ti = -ti
    col_w[0:LANES, 0:LANES] = tr.astype(BF16)
    col_w[0:LANES, LANES:] = ti.astype(BF16)
    col_w[LANES:, 0:LANES] = (-ti).astype(BF16)
    col_w[LANES:, LANES:] = tr.astype(BF16)
    freq_b = wrap(column + COL_STEP * iota((BLOCKS, LANES), 1))
    wr, wi = cis(freq_b * wrap(b + LANES * iota((BLOCKS, LANES), 0)))
    tw_r[...] = wr
    tw_i[...] = wi

    acc_r = jnp.zeros((ROWS_DEV, LANES), F32)
    acc_i = jnp.zeros((ROWS_DEV, LANES), F32)
    width = BLOCKS // PARTS
    for part in range(PARTS):
        load[part].wait()
        for y in range(width * part, width * (part + 1)):
            rows = slice(ROWS_DEV * y, ROWS_DEV * (y + 1))
            lanes = slice(LANES * y, LANES * (y + 1))
            wide[rows, 0:LANES] = facet_v[0:ROWS_DEV, lanes]
            wide[rows, LANES:] = facet_v[ROWS_DEV:, lanes]
        rows = slice(ROWS_DEV * width * part, ROWS_DEV * width * (part + 1))
        prod = dot(wide[rows, :], col_w[...])
        for k in range(width):
            y = width * part + k
            rows = slice(ROWS_DEV * k, ROWS_DEV * (k + 1))
            dr, di = prod[rows, 0:LANES], prod[rows, LANES:]
            cr, ci = tw_r[y : y + 1, :], tw_i[y : y + 1, :]
            acc_r += dr * cr + di * ci
            acc_i += di * cr - dr * ci
    transformed = jnp.concatenate([acc_r, acc_i], 1) * (1.0 / math.sqrt(FACET_W))
    gath[q] = transformed.astype(BF16)

    pl.semaphore_wait(barrier, len(greeted) + FREQS - 1)
    copies_a = [
        send(0, i, gath.at[q], gath.at[q], {"freq": peer}) for i, peer in enumerate(freq_peers)
    ]

    place = wrap(a + iota((8, FACET_ROWS), 1))
    coarse = cis(8 * ROW_STEP * iota((16, FACET_ROWS), 0) * wrap(a + iota((16, FACET_ROWS), 1)))
    for n, start in enumerate(starts):
        fine = cis(wrap(start + ROW_STEP * iota((8, FACET_ROWS), 0)) * place)
        rr, ri = outer(fine, coarse)
        first = 2 * PAIR * (n // OWN) + CONTRIB * (n % OWN)
        for z in range(2):
            lanes = slice(HALF * z, HALF * (z + 1))
            row_t[z, first : first + CONTRIB, :] = rr[:, lanes].astype(BF16)
            row_t[z, PAIR + first : PAIR + first + CONTRIB, :] = (-ri[:, lanes]).astype(BF16)

    lane_k = iota((8, CONTRIB), 1)
    fine = cis(iota((8, CONTRIB), 0) * wrap(STEP * lane_k + a))
    coarse = cis(8 * iota((32, CONTRIB), 0) * wrap(STEP * iota((32, CONTRIB), 1) + a))
    sr, si = outer(fine, coarse)
    for g in range(SIDE):
        rows = slice(PATCH * g, PATCH * (g + 1))
        half = PATCH * (g // 4)
        spread_t[g % 4, half : half + PATCH, :] = sr[rows].astype(BF16)
        spread_t[g % 4, 2 * PATCH + half : 3 * PATCH + half, :] = si[rows].astype(BF16)

    fine = cis(STEP * iota((8, SUBGRID), 0) * iota((8, SUBGRID), 1))
    coarse = cis(8 * STEP * iota((16, SUBGRID), 0) * iota((16, SUBGRID), 1))
    gr, gi = outer(fine, coarse)
    grid_w[0:CONTRIB, 0:SUBGRID] = gr.astype(BF16)
    grid_w[0:CONTRIB, SUBGRID:] = gi.astype(BF16)
    grid_w[CONTRIB:, 0:SUBGRID] = (-gi).astype(BF16)
    grid_w[CONTRIB:, SUBGRID:] = gr.astype(BF16)

    shift_b = jnp.concatenate(
        [jnp.full((1, SUBGRID), offs_s[1, g], jnp.int32) for g in range(FACETS)], 0
    )
    pr, pi = cis(iota((FACETS, SUBGRID), 1) * shift_b)
    ph_r[...] = pr
    ph_i[...] = pi

    def own_half(z):
        return dot(row_t[z], gath[pl.ds(8 * z, 8)].reshape(HALF, PAIR))

    for copy, step in zip(copies_a, FREQ_STEPS):
        if step[0] == 0:
            copy.wait_recv()
    both = own_half(q // 8)
    for copy, step in zip(copies_a, FREQ_STEPS):
        if step[0] == 1:
            copy.wait_recv()
    both += own_half(1 - q // 8)
    contribs = []
    for e in range(2):
        top, low = both[2 * PAIR * e : 2 * PAIR * e + PAIR], both[2 * PAIR * e + PAIR : 2 * PAIR * (e + 1)]
        cr = top[:, 0:CONTRIB] - low[:, CONTRIB:]
        ci = top[:, CONTRIB:] + low[:, 0:CONTRIB]
        contrib = (jnp.concatenate([cr, ci], 1) * (1.0 / math.sqrt(FACET_ROWS))).astype(BF16)
        contribs.append(jnp.concatenate([contrib[0:CONTRIB], contrib[CONTRIB:]], 1))
    copies_b = []
    for d in (3, 2, 1, 0):
        both = dot(spread_t[target(d)], contribs[d % 2])
        for j in range(OWN):
            re, im = slice(PAIR * j, PAIR * j + CONTRIB), slice(PAIR * j + CONTRIB, PAIR * (j + 1))
            sr = both[0 : 2 * PATCH, re] - both[2 * PATCH :, im]
            si = both[0 : 2 * PATCH, im] + both[2 * PATCH :, re]
            part = jnp.concatenate([sr, si], 1).astype(BF16)
            send_b[4 * d + 2 * j] = part[0:PATCH]
            send_b[4 * d + 2 * j + 1] = part[PATCH:]
        for i, step in enumerate(SPREAD_STEPS):
            if step[1] == d:
                src = send_b.at[4 * d + lax.rem(x + step[0], 4)]
                copies_b.append(send(1, i, src, recv_b.at[f], beside(step[0], d)))
    recv_b[f] = send_b[x]

    load_uv.wait()
    load_seen.wait()

    def patch_rows(coords):
        cell = iota((8, VIS), 0)
        by8 = cis(8 * coords, PERIOD)
        by16 = cis(16 * coords, PERIOD)
        for c in range(SIDE):
            row = jnp.broadcast_to(coords[c : c + 1], (8, VIS))
            low = cis(cell * row, PERIOD)
            mid = cmul(low, (by8[0][c : c + 1], by8[1][c : c + 1]))
            half = (jnp.concatenate([low[0], mid[0]], 0), jnp.concatenate([low[1], mid[1]], 0))
            high = cmul(half, (by16[0][c : c + 1], by16[1][c : c + 1]))
            yield (
                c,
                jnp.concatenate([half[0], high[0]], 0),
                jnp.concatenate([half[1], high[1]], 0),
            )

    for c, er, ei in patch_rows(uv_v[0:SIDE, :]):
        eu_r[PATCH * c : PATCH * (c + 1), :] = er
        eu_i[PATCH * c : PATCH * (c + 1), :] = ei
    for c, er, ei in patch_rows(uv_v[SIDE:, :]):
        first = PATCH * (c % 4)
        ev[c // 4, first : first + PATCH, :] = er.astype(BF16)
        ev[c // 4, LANES + first : LANES + first + PATCH, :] = ei.astype(BF16)

    fine = cis(STEP * iota((8, CONTRIB), 0) * lane_k)
    coarse = cis(8 * STEP * iota((32, CONTRIB), 0) * iota((32, CONTRIB), 1))
    nr, ni = outer(fine, coarse)
    narrow_w[0:SUBGRID, 0:CONTRIB] = nr.astype(BF16)
    narrow_w[0:SUBGRID, CONTRIB:] = (-ni).astype(BF16)
    narrow_w[SUBGRID:, 0:CONTRIB] = ni.astype(BF16)
    narrow_w[SUBGRID:, CONTRIB:] = nr.astype(BF16)

    for z in range(4):

        def cell(rows):
            lane = iota((rows, 2 * PATCH), 1)
            block = 4 * lax.shift_right_logical(lane, 5) + z
            return PATCH * block + (lane & (PATCH - 1))

        fine = cis(wrap(STEP * iota((8, 2 * PATCH), 0) + a) * cell(8))
        coarse = cis(8 * STEP * iota((16, 2 * PATCH), 0) * cell(16))
        hr, hi = outer(fine, coarse)
        spread_h[z, 0:CONTRIB, :] = hr.astype(BF16)
        spread_h[z, CONTRIB:, :] = (-hi).astype(BF16)

    def own_freq(rows):
        lane = iota((rows, 2 * PAIR), 1)
        which = lax.shift_right_logical(lane, 7)
        start = jnp.where(which == 0, starts[0], starts[1])
        start = jnp.where(which == 2, starts[2], start)
        start = jnp.where(which == 3, starts[3], start)
        return wrap(start + ROW_STEP * (lane & (CONTRIB - 1)))

    fine = cis(own_freq(8) * wrap(a + iota((8, 2 * PAIR), 0)))
    coarse = cis(own_freq(FACET_ROWS // 8) * (8 * iota((FACET_ROWS // 8, 2 * PAIR), 0)))
    hr, hi = outer(fine, coarse)
    for z in range(2):
        rows = slice(HALF * z, HALF * (z + 1))
        row_h[z, 0:HALF, :] = hr[rows].astype(BF16)
        row_h[z, HALF:, :] = hi[rows].astype(BF16)

    fine = cis(wrap(column + COL_STEP * iota((8, LANES), 0)) * iota((8, LANES), 1))
    coarse = cis(8 * COL_STEP * iota((16, LANES), 0) * iota((16, LANES), 1))
    br, bi = outer(fine, coarse)
    back_w[0:LANES, 0:LANES] = br.astype(BF16)
    back_w[0:LANES, LANES:] = bi.astype(BF16)
    back_w[LANES:, 0:LANES] = (-bi).astype(BF16)
    back_w[LANES:, LANES:] = br.astype(BF16)

    grid_r = jnp.zeros((PATCH, SUBGRID), F32)
    grid_i = jnp.zeros((PATCH, SUBGRID), F32)
    for d in range(4):
        for copy, step in zip(copies_b, SPREAD_STEPS):
            if step[1] == d:
                copy.wait_recv()
        senders = [4 * col + origin(d) for col in range(4)]
        rows = jnp.concatenate([recv_b[g] for g in senders], 0)
        part = dot(rows, grid_w[...])
        for n, g in enumerate(senders):
            rows = slice(PATCH * n, PATCH * (n + 1))
            qr, qi = part[rows, 0:SUBGRID], part[rows, SUBGRID:]
            pr, pi = ph_r[pl.ds(g, 1), :], ph_i[pl.ds(g, 1), :]
            grid_r += qr * pr - qi * pi
            grid_i += qr * pi + qi * pr
    grid_r = grid_r * (1.0 / CONTRIB)
    grid_i = grid_i * (1.0 / CONTRIB)

    patch_of = lax.shift_right_logical(iota((PATCH, LANES), 1), 5)
    for c in range(SIDE):
        mine = patch_of == c % 4
        lanes = slice(LANES * (c // 4), LANES * (c // 4 + 1))
        gr = jnp.where(mine, grid_r[:, lanes], 0.0)
        gi = jnp.where(mine, grid_i[:, lanes], 0.0)
        first = PATCH * (c % 4)
        rows = slice(first, first + PATCH)
        low = slice(LANES + first, LANES + first + PATCH)
        cells[c // 4, rows, 0:LANES] = gr.astype(BF16)
        cells[c // 4, rows, LANES:] = (-gi).astype(BF16)
        cells[c // 4, low, 0:LANES] = gi.astype(BF16)
        cells[c // 4, low, LANES:] = gr.astype(BF16)
    models_r, models_i = [], []
    for h in range(2):
        quad[h] = dot(cells[h], ev[h])
    for c in range(SIDE):
        first = PATCH * (c % 4)
        inner_r = quad[c // 4, first : first + PATCH, :]
        inner_i = quad[c // 4, LANES + first : LANES + first + PATCH, :]
        ur, ui = eu_r[PATCH * c : PATCH * (c + 1), :], eu_i[PATCH * c : PATCH * (c + 1), :]
        models_r.append(jnp.sum(ur * inner_r - ui * inner_i, axis=0, keepdims=True))
        models_i.append(jnp.sum(ur * inner_i + ui * inner_r, axis=0, keepdims=True))
    model = jnp.concatenate(models_r + models_i, 0) * (1.0 / PATCH)
    residual = (seen_v[...].astype(F32) - model).astype(BF16)
    res_out[...] = residual
    residual = residual.astype(F32)
    backs_r, backs_i = [], []
    for h in range(2):
        for c in range(4 * h, 4 * (h + 1)):
            first = PATCH * (c % 4)
            rr, ri = residual[c : c + 1, :], residual[SIDE + c : SIDE + c + 1, :]
            ur, ui = eu_r[PATCH * c : PATCH * (c + 1), :], eu_i[PATCH * c : PATCH * (c + 1), :]
            weigh[h, first : first + PATCH, :] = (rr * ur + ri * ui).astype(BF16)
            weigh[h, LANES + first : LANES + first + PATCH, :] = (ri * ur - rr * ui).astype(BF16)
        full = lax.dot_general(
            weigh[h], ev[h], (((1,), (1,)), ((), ())), preferred_element_type=F32
        )
        back_r = jnp.zeros((PATCH, LANES), F32)
        back_i = jnp.zeros((PATCH, LANES), F32)
        for c in range(4):
            mine = patch_of == c
            rows = slice(PATCH * c, PATCH * (c + 1))
            low = slice(LANES + PATCH * c, LANES + PATCH * (c + 1))
            back_r = jnp.where(mine, full[rows, 0:LANES] + full[low, LANES:], back_r)
            back_i = jnp.where(mine, full[low, 0:LANES] - full[rows, LANES:], back_i)
        backs_r.append(back_r)
        backs_i.append(back_i)
    back_r = jnp.concatenate(backs_r, 1)
    back_i = jnp.concatenate(backs_i, 1)
    back_r = back_r * (1.0 / math.sqrt(VIS))
    back_i = back_i * (1.0 / math.sqrt(VIS))

    copies_c = []
    for d in (3, 2, 1, 0):
        for n in range(4):
            g = 4 * n + origin(d)
            rows = slice(PATCH * n, PATCH * (n + 1))
            pr, pi = ph_r[pl.ds(g, 1), :], ph_i[pl.ds(g, 1), :]
            shifted[d, rows, 0:SUBGRID] = (back_r * pr + back_i * pi).astype(BF16)
            shifted[d, rows, SUBGRID:] = (back_i * pr - back_r * pi).astype(BF16)
        narrowed = dot(shifted[d], narrow_w[...]).astype(BF16)
        send_c[4 * d : 4 * (d + 1)] = narrowed.reshape(4, PATCH, PAIR)
        for i, step in enumerate(SPREAD_STEPS):
            if step[1] == d:
                src = send_c.at[4 * d + lax.rem(x + step[0], 4)]
                device = beside(step[0], back_step(d))
                copies_c.append(send(2, i, src, recv_c.at[4 * d + x], device))
    recv_c[x] = send_c[x]

    halves = [None, None]
    for d in range(4):
        for copy, step in zip(copies_c, SPREAD_STEPS):
            if step[1] == d:
                copy.wait_recv()
        rows = jnp.concatenate(
            [recv_c[4 * d + 2 * j : 4 * d + 2 * j + 2].reshape(2 * PATCH, PAIR) for j in range(OWN)], 1
        )
        part = dot(spread_h[target(d)], rows)
        halves[d % 2] = part if d < 2 else halves[d % 2] + part
    adjoint = []
    for both in halves:
        for j in range(OWN):
            re, im = slice(PAIR * j, PAIR * j + CONTRIB), slice(PAIR * j + CONTRIB, PAIR * (j + 1))
            ar = both[0:CONTRIB, re] - both[CONTRIB:, im]
            ai = both[0:CONTRIB, im] + both[CONTRIB:, re]
            adjoint.append((jnp.concatenate([ar, ai], 1) * (1.0 / SUBGRID)).astype(BF16))
    adjoint = jnp.concatenate(adjoint, 0)
    copies_d = []
    for dz in (1, 0):
        z = lax.rem(q // 8 + dz, 2)
        both = dot(row_h[z], adjoint)
        rr = both[0:HALF, 0:CONTRIB] - both[HALF:, CONTRIB:]
        ri = both[0:HALF, CONTRIB:] + both[HALF:, 0:CONTRIB]
        rows = jnp.concatenate([rr, ri], 1).astype(BF16)
        send_d[pl.ds(8 * z, 8)] = rows.reshape(8, ROWS_DEV, PAIR)
        copies_d += [
            send(3, i, send_d.at[peer], recv_d.at[q], {"freq": peer}) for i, peer in freq_group(dz)
        ]

    total = send_d[q].astype(F32)
    order_d = [FREQ_STEPS[i] for dz in (1, 0) for i, _ in freq_group(dz)]
    for copy, step in list(zip(copies_d, order_d))[::-1]:
        copy.wait_recv()
        total += recv_d[freq_peer(q, (-step[0] % 2, -step[1] % 4, -step[2] % 2))].astype(F32)
    total = total * (1.0 / (math.sqrt(SUBGRIDS * CONTRIB) * math.sqrt(CONTRIB)))
    total_out[...] = total
    for copies in (copies_a, copies_b, copies_c, copies_d):
        for copy in copies:
            copy.wait_send()


def finish(total, tw_r, tw_i, back_w, residual, img_out, res_out, wide, image, out_sem):
    stores = [pltpu.make_async_copy(residual, res_out, out_sem.at[PARTS])]
    stores[0].start()
    tot_r, tot_i = total[:, 0:CONTRIB], total[:, CONTRIB:]
    for part in range(PARTS):
        width = BLOCKS // PARTS
        for y in range(width * part, width * (part + 1)):
            rows = slice(ROWS_DEV * y, ROWS_DEV * (y + 1))
            cr, ci = tw_r[y : y + 1, :], tw_i[y : y + 1, :]
            wide[rows, 0:LANES] = (tot_r * cr - tot_i * ci).astype(BF16)
            wide[rows, LANES:] = (tot_r * ci + tot_i * cr).astype(BF16)
        rows = slice(ROWS_DEV * width * part, ROWS_DEV * width * (part + 1))
        prod = dot(wide[rows, :], back_w[...]).astype(BF16)
        for k in range(width):
            lanes = slice(LANES * (width * part + k), LANES * (width * part + k + 1))
            rows = slice(ROWS_DEV * k, ROWS_DEV * (k + 1))
            image[0:ROWS_DEV, lanes] = prod[rows, 0:LANES]
            image[ROWS_DEV:, lanes] = prod[rows, LANES:]
        lanes = pl.ds(LANES * width * part, LANES * width)
        store = pltpu.make_async_copy(image.at[:, lanes], img_out.at[:, lanes], out_sem.at[part])
        store.start()
        stores.append(store)
    for store in stores:
        store.wait()


def in_hbm(x):
    return pltpu.with_memory_space_constraint(x, pltpu.HBM)


def on_device(facet_image, facet_offsets, subgrid_rows, column_offset, uv_coords, observed):
    vmem = pl.BlockSpec(memory_space=pltpu.VMEM)
    smem = pl.BlockSpec(memory_space=pltpu.SMEM)
    hbm = pl.BlockSpec(memory_space=pltpu.HBM)
    chunk = pltpu.VMEM((16, 32, PAIR), BF16)
    *middle, residual = pl.pallas_call(
        kernel,
        out_shape=(
            jax.ShapeDtypeStruct((ROWS_DEV, PAIR), F32),
            jax.ShapeDtypeStruct((BLOCKS, LANES), F32),
            jax.ShapeDtypeStruct((BLOCKS, LANES), F32),
            jax.ShapeDtypeStruct((PAIR, PAIR), BF16),
            jax.ShapeDtypeStruct((2 * SIDE, VIS), BF16),
        ),
        in_specs=[hbm, hbm, smem, hbm, hbm, hbm],
        out_specs=(vmem,) * 5,
        scratch_shapes=[
            pltpu.SMEM((2, FACETS), jnp.int32),
            pltpu.SMEM((SUBGRIDS,), jnp.int32),
            pltpu.VMEM((2 * ROWS_DEV, FACET_W), BF16),
            pltpu.VMEM((2 * SIDE, VIS), jnp.int32),
            pltpu.VMEM((2 * SIDE, VIS), BF16),
            pltpu.VMEM((BLOCKS * ROWS_DEV, PAIR), BF16),
            pltpu.VMEM((PAIR, PAIR), BF16),
            pltpu.VMEM((2, 4 * PAIR, HALF), BF16),
            pltpu.VMEM((2, 2 * HALF, 2 * PAIR), BF16),
            pltpu.VMEM((4, 4 * PATCH, CONTRIB), BF16),
            pltpu.VMEM((4, 2 * CONTRIB, 2 * PATCH), BF16),
            pltpu.VMEM((PAIR, 2 * SUBGRID), BF16),
            pltpu.VMEM((2 * SUBGRID, PAIR), BF16),
            pltpu.VMEM((FACETS, SUBGRID), F32),
            pltpu.VMEM((FACETS, SUBGRID), F32),
            pltpu.VMEM((SUBGRID, VIS), F32),
            pltpu.VMEM((SUBGRID, VIS), F32),
            pltpu.VMEM((2, SUBGRID, VIS), BF16),
            pltpu.VMEM((2, SUBGRID, VIS), F32),
            pltpu.VMEM((2, SUBGRID, SUBGRID), BF16),
            pltpu.VMEM((2, SUBGRID, VIS), BF16),
            pltpu.VMEM((4, 4 * PATCH, 2 * SUBGRID), BF16),
            chunk,
            chunk,
            chunk,
            chunk,
            chunk,
            chunk,
            chunk,
            pltpu.SemaphoreType.DMA((6,)),
            pltpu.SemaphoreType.DMA((PARTS,)),
            pltpu.SemaphoreType.DMA((4, 15)),
            pltpu.SemaphoreType.DMA((4, 15)),
        ],
        compiler_params=pltpu.CompilerParams(
            collective_id=0, has_side_effects=True, vmem_limit_bytes=24 * 1024 * 1024
        ),
    )(
        in_hbm(facet_offsets.T),
        in_hbm(subgrid_rows),
        column_offset,
        in_hbm(facet_image.reshape(2 * ROWS_DEV, FACET_W)),
        in_hbm(uv_coords.reshape(2 * SIDE, VIS)),
        in_hbm(observed.reshape(2 * SIDE, VIS)),
    )
    image, residual = pl.pallas_call(
        finish,
        out_shape=(
            jax.ShapeDtypeStruct((2 * ROWS_DEV, FACET_W), BF16),
            jax.ShapeDtypeStruct((2 * SIDE, VIS), BF16),
        ),
        in_specs=[vmem] * 5,
        out_specs=(hbm, hbm),
        scratch_shapes=[
            pltpu.VMEM((BLOCKS * ROWS_DEV, PAIR), BF16),
            pltpu.VMEM((2 * ROWS_DEV, FACET_W), BF16),
            pltpu.SemaphoreType.DMA((PARTS + 1,)),
        ],
        compiler_params=pltpu.CompilerParams(vmem_limit_bytes=24 * 1024 * 1024),
    )(*middle, residual)
    return (
        image.reshape(1, 2, ROWS_DEV, FACET_W),
        residual.reshape(2, 1, SIDE, VIS),
    )


def solution(mesh):
    return jax.shard_map(
        on_device,
        mesh=mesh,
        in_specs=(
            P("facet", None, "freq", None),
            P(),
            P(),
            P(),
            P(None, ("freq", "facet"), None, None),
            P(None, ("freq", "facet"), None, None),
        ),
        out_specs=(P("facet", None, "freq", None), P(None, ("freq", "facet"), None, None)),
        check_vma=False,
    )
```

```python
import math

import jax
import jax.numpy as jnp
from jax import lax
from jax.experimental import pallas as pl
from jax.experimental.pallas import tpu as pltpu
from jax.sharding import PartitionSpec as P

IMAGE = 32768
CONTRIB = 128
SUBGRID = 256
PATCH = 32
SIDE = 8
PERIOD = 256
COL_STEP = 8
ROW_STEP = 64
STEP = 128
FACETS = 16
FREQS = 16
ROWS_DEV = 32
FACET_ROWS = FREQS * ROWS_DEV
FACET_W = 4096
SUBGRIDS = 32
OWN = 2
VIS = 512
LANES = 128
BLOCKS = FACET_W // LANES
PAIR = 2 * CONTRIB
PARTS = 4
HALF = FACET_ROWS // 2

TWO_PI = 2.0 * math.pi
MESH = pl.DeviceIdType.MESH
F32 = jnp.float32
BF16 = jnp.bfloat16


def ring_hops(step, size):
    return min(step, size - step)


SPREAD_STEPS = [(x, d) for d in (3, 1, 2, 0) for x in (2, 1, 3, 0) if x or d]
FREQ_STEPS = sorted(
    [(z, y, c) for z in range(2) for y in range(4) for c in range(2) if z or y or c],
    key=lambda s: -s[0] - ring_hops(s[1], 4),
)


def freq_peer(q, step):
    z, y, c = q // 8, lax.rem(q // 2, 4), lax.rem(q, 2)
    return (lax.rem(z + step[0], 2) * 4 + lax.rem(y + step[1], 4)) * 2 + lax.rem(c + step[2], 2)


def back_step(d):
    return d if d % 2 else -d


def iota(shape, dim):
    return lax.broadcasted_iota(jnp.int32, shape, dim)


def wrap(m):
    return m & (IMAGE - 1)


def cis(m, period=IMAGE):
    quarter = period // 4
    m = m & (period - 1)
    turn = lax.shift_right_logical(m + quarter // 2, int(math.log2(quarter)))
    rest = (m - turn * quarter).astype(F32) * (TWO_PI / period)
    sq = rest * rest
    sin = 1.0 / 120.0 + sq * (-1.0 / 5040.0 + sq * (1.0 / 362880.0))
    sin = rest + rest * (sq * (-1.0 / 6.0 + sq * sin))
    cos = 1.0 / 24.0 + sq * (-1.0 / 720.0 + sq * (1.0 / 40320.0))
    cos = 1.0 + sq * (-0.5 + sq * cos)
    odd = (turn & 1) == 1
    c = jnp.where(odd, sin, cos)
    s = jnp.where(odd, cos, sin)
    c = jnp.where(((turn + 1) & 2) == 2, -c, c)
    s = jnp.where((turn & 2) == 2, -s, s)
    return c, s


def cmul(a, b):
    return a[0] * b[0] - a[1] * b[1], a[0] * b[1] + a[1] * b[0]


def outer(fine, coarse):
    rows = [
        cmul(fine, (coarse[0][h : h + 1], coarse[1][h : h + 1])) for h in range(coarse[0].shape[0])
    ]
    return jnp.concatenate([r[0] for r in rows], 0), jnp.concatenate([r[1] for r in rows], 0)


def with_turned(t):
    turned = []
    for first in range(0, t.shape[1], PAIR):
        turned += [-t[:, first + CONTRIB : first + PAIR], t[:, first : first + CONTRIB]]
    return jnp.concatenate([t, jnp.concatenate(turned, 1)], 0)


def dot(a, b):
    return jnp.dot(a, b, preferred_element_type=F32)


def kernel(
    offs_in,
    starts_in,
    col_s,
    facet_in,
    uv_in,
    seen_in,
    total_out,
    tw_r,
    tw_i,
    back_w,
    res_out,
    offs_s,
    starts_s,
    facet_v,
    uv_v,
    seen_v,
    wide,
    col_w,
    row_t,
    row_h,
    spread_t,
    spread_h,
    grid_w,
    narrow_w,
    ph_r,
    ph_i,
    eu_r,
    eu_i,
    ev,
    quad,
    cells,
    weigh,
    shifted,
    gath,
    send_b,
    recv_b,
    send_c,
    recv_c,
    send_d,
    recv_d,
    in_sem,
    load_sem,
    tx_sem,
    rx_sem,
):
    f = lax.axis_index("facet")
    q = lax.axis_index("freq")

    loads = [
        pltpu.make_async_copy(src, dst, in_sem.at[3 + i])
        for i, (src, dst) in enumerate(
            ((offs_in, offs_s), (starts_in, starts_s))
        )
    ]
    for copy in loads:
        copy.start()
    load = []
    for i in range(PARTS):
        lanes = pl.ds(FACET_W // PARTS * i, FACET_W // PARTS)
        load.append(
            pltpu.make_async_copy(
                facet_in.at[:, lanes], facet_v.at[:, lanes], load_sem.at[i]
            )
        )
        load[i].start()
    load_uv = pltpu.make_async_copy(uv_in, uv_v, in_sem.at[1])
    load_uv.start()
    load_seen = pltpu.make_async_copy(seen_in, seen_v, in_sem.at[2])
    load_seen.start()

    barrier = pltpu.get_barrier_semaphore()
    x, chip, other = f // 4, 2 * lax.rem(f, 4) + q // 8, lax.rem(q + 8, FREQS)
    away = 2 * (q // 8) - 1

    def beside(dx, dz):
        z = lax.rem(chip + away * dz + 8, 8)
        return {"facet": 4 * lax.rem(x + dx, 4) + z // 2, "freq": other if dz % 2 else q}

    def target(d):
        return lax.rem(chip + away * d + 8, 8) // 2

    def origin(d):
        return lax.rem(chip + away * back_step(d) + 8, 8) // 2

    freq_peers = [freq_peer(q, step) for step in FREQ_STEPS]
    greeted = [(dx, dz) for dx in range(4) for dz in (0, 1, 2, 3, -2) if dx or dz]
    for dx, dz in greeted:
        pl.semaphore_signal(barrier, inc=1, device_id=beside(dx, dz), device_id_type=MESH)
    for peer in freq_peers:
        pl.semaphore_signal(barrier, inc=1, device_id={"freq": peer}, device_id_type=MESH)

    for copy in loads:
        copy.wait()
    a = offs_s[0, f]
    b = offs_s[1, f]
    column = col_s[0]
    starts = [starts_s[OWN * who + j] for who in (q, other) for j in range(OWN)]

    def freq_group(dz):
        return [(i, p) for i, p in enumerate(freq_peers) if FREQ_STEPS[i][0] == dz]

    def send(stage, i, src, dst, device):
        copy = pltpu.make_async_remote_copy(
            src_ref=src,
            dst_ref=dst,
            send_sem=tx_sem.at[stage, i],
            recv_sem=rx_sem.at[stage, i],
            device_id=device,
            device_id_type=MESH,
        )
        copy.start()
        return copy

    freq_l = wrap(column + COL_STEP * iota((8, LANES), 1))
    fine = cis(freq_l * iota((8, LANES), 0))
    freq_h = wrap(column + COL_STEP * iota((16, LANES), 1))
    coarse = cis(freq_h * (8 * iota((16, LANES), 0)))
    tr, ti = outer(fine, coarse)
    ti = -ti
    col_w[0:LANES, 0:LANES] = tr.astype(BF16)
    col_w[0:LANES, LANES:] = ti.astype(BF16)
    col_w[LANES:, 0:LANES] = (-ti).astype(BF16)
    col_w[LANES:, LANES:] = tr.astype(BF16)
    freq_b = wrap(column + COL_STEP * iota((BLOCKS, LANES), 1))
    wr, wi = cis(freq_b * wrap(b + LANES * iota((BLOCKS, LANES), 0)))
    tw_r[...] = wr
    tw_i[...] = wi

    acc_r = jnp.zeros((ROWS_DEV, LANES), F32)
    acc_i = jnp.zeros((ROWS_DEV, LANES), F32)
    for y in range(BLOCKS):
        if y % (BLOCKS // PARTS) == 0:
            load[y // (BLOCKS // PARTS)].wait()
        rows = slice(ROWS_DEV * y, ROWS_DEV * (y + 1))
        lanes = slice(LANES * y, LANES * (y + 1))
        wide[rows, 0:LANES] = facet_v[0:ROWS_DEV, lanes]
        wide[rows, LANES:] = facet_v[ROWS_DEV:, lanes]
    width = BLOCKS // 1
    for part in range(1):
        rows = slice(ROWS_DEV * width * part, ROWS_DEV * width * (part + 1))
        prod = dot(wide[rows, :], col_w[...])
        for k in range(width):
            y = width * part + k
            rows = slice(ROWS_DEV * k, ROWS_DEV * (k + 1))
            dr, di = prod[rows, 0:LANES], prod[rows, LANES:]
            cr, ci = tw_r[y : y + 1, :], tw_i[y : y + 1, :]
            acc_r += dr * cr + di * ci
            acc_i += di * cr - dr * ci
    transformed = jnp.concatenate([acc_r, acc_i], 1) * (1.0 / math.sqrt(FACET_W))
    gath[q] = transformed.astype(BF16)

    pl.semaphore_wait(barrier, len(greeted) + FREQS - 1)
    copies_a = [
        send(0, i, gath.at[q], gath.at[q], {"freq": peer}) for i, peer in enumerate(freq_peers)
    ]

    place = wrap(a + iota((8, FACET_ROWS), 1))
    coarse = cis(8 * ROW_STEP * iota((16, FACET_ROWS), 0) * wrap(a + iota((16, FACET_ROWS), 1)))
    for n, start in enumerate(starts):
        fine = cis(wrap(start + ROW_STEP * iota((8, FACET_ROWS), 0)) * place)
        rr, ri = outer(fine, coarse)
        rows = slice(CONTRIB * n, CONTRIB * (n + 1))
        for z in range(2):
            lanes = slice(HALF * z, HALF * (z + 1))
            row_t[z, rows, 0:HALF] = rr[:, lanes].astype(BF16)
            row_t[z, rows, HALF:] = (-ri[:, lanes]).astype(BF16)

    lane_k = iota((8, CONTRIB), 1)
    fine = cis(iota((8, CONTRIB), 0) * wrap(STEP * lane_k + a))
    coarse = cis(8 * iota((32, CONTRIB), 0) * wrap(STEP * iota((32, CONTRIB), 1) + a))
    sr, si = outer(fine, coarse)
    for g in range(SIDE):
        rows = slice(PATCH * g, PATCH * (g + 1))
        half = PATCH * (g // 4)
        spread_t[g % 4, half : half + PATCH, 0:CONTRIB] = sr[rows].astype(BF16)
        spread_t[g % 4, half : half + PATCH, CONTRIB:] = si[rows].astype(BF16)

    fine = cis(STEP * iota((8, SUBGRID), 0) * iota((8, SUBGRID), 1))
    coarse = cis(8 * STEP * iota((16, SUBGRID), 0) * iota((16, SUBGRID), 1))
    gr, gi = outer(fine, coarse)
    grid_w[0:CONTRIB, 0:SUBGRID] = gr.astype(BF16)
    grid_w[0:CONTRIB, SUBGRID:] = gi.astype(BF16)
    grid_w[CONTRIB:, 0:SUBGRID] = (-gi).astype(BF16)
    grid_w[CONTRIB:, SUBGRID:] = gr.astype(BF16)

    shift_b = jnp.concatenate(
        [jnp.full((1, SUBGRID), offs_s[1, g], jnp.int32) for g in range(FACETS)], 0
    )
    pr, pi = cis(iota((FACETS, SUBGRID), 1) * shift_b)
    ph_r[...] = pr
    ph_i[...] = pi

    def own_half(z):
        return dot(row_t[z], with_turned(gath[pl.ds(8 * z, 8)].reshape(HALF, PAIR)))

    for copy, step in zip(copies_a, FREQ_STEPS):
        if step[0] == 0:
            copy.wait_recv()
    both = own_half(q // 8)
    for copy, step in zip(copies_a, FREQ_STEPS):
        if step[0] == 1:
            copy.wait_recv()
    both += own_half(1 - q // 8)
    contrib = (both * (1.0 / math.sqrt(FACET_ROWS))).astype(BF16)
    copies_b = []
    for pair in ((3, 1), (2, 0)):
        first = PAIR * (pair[0] % 2)
        rows = slice(first, first + CONTRIB), slice(first + CONTRIB, first + PAIR)
        own = with_turned(jnp.concatenate([contrib[r] for r in rows], 1))
        table = jnp.concatenate([spread_t[target(d)] for d in pair], 0)
        parts = dot(table, own).astype(BF16)
        for n, d in enumerate(pair):
            for j in range(OWN):
                for half in range(2):
                    first = PATCH * (2 * n + half)
                    part = parts[first : first + PATCH, PAIR * j : PAIR * (j + 1)]
                    send_b[4 * d + 2 * j + half] = part
            for i, step in enumerate(SPREAD_STEPS):
                if step[1] == d:
                    src = send_b.at[4 * d + lax.rem(x + step[0], 4)]
                    copies_b.append(send(1, i, src, recv_b.at[f], beside(step[0], d)))
    recv_b[f] = send_b[x]

    load_uv.wait()
    load_seen.wait()

    def patch_rows(coords):
        cell = iota((8, VIS), 0)
        by8 = cis(8 * coords, PERIOD)
        by16 = cis(16 * coords, PERIOD)
        for c in range(SIDE):
            row = jnp.broadcast_to(coords[c : c + 1], (8, VIS))
            low = cis(cell * row, PERIOD)
            mid = cmul(low, (by8[0][c : c + 1], by8[1][c : c + 1]))
            half = (jnp.concatenate([low[0], mid[0]], 0), jnp.concatenate([low[1], mid[1]], 0))
            high = cmul(half, (by16[0][c : c + 1], by16[1][c : c + 1]))
            yield (
                c,
                jnp.concatenate([half[0], high[0]], 0),
                jnp.concatenate([half[1], high[1]], 0),
            )

    for c, er, ei in patch_rows(uv_v[0:SIDE, :]):
        eu_r[PATCH * c : PATCH * (c + 1), :] = er
        eu_i[PATCH * c : PATCH * (c + 1), :] = ei
    for c, er, ei in patch_rows(uv_v[SIDE:, :]):
        first = PATCH * (c % 4)
        ev[c // 4, first : first + PATCH, :] = er.astype(BF16)
        ev[c // 4, LANES + first : LANES + first + PATCH, :] = ei.astype(BF16)

    fine = cis(STEP * iota((8, CONTRIB), 0) * lane_k)
    coarse = cis(8 * STEP * iota((32, CONTRIB), 0) * iota((32, CONTRIB), 1))
    nr, ni = outer(fine, coarse)
    narrow_w[0:SUBGRID, 0:CONTRIB] = nr.astype(BF16)
    narrow_w[0:SUBGRID, CONTRIB:] = (-ni).astype(BF16)
    narrow_w[SUBGRID:, 0:CONTRIB] = ni.astype(BF16)
    narrow_w[SUBGRID:, CONTRIB:] = nr.astype(BF16)

    for z in range(4):

        def cell(rows):
            lane = iota((rows, 4 * PATCH), 1) & (2 * PATCH - 1)
            block = 4 * lax.shift_right_logical(lane, 5) + z
            return PATCH * block + (lane & (PATCH - 1))

        fine = cis(wrap(STEP * iota((8, 4 * PATCH), 0) + a) * cell(8))
        coarse = cis(8 * STEP * iota((16, 4 * PATCH), 0) * cell(16))
        hr, hi = outer(fine, coarse)
        real = iota((CONTRIB, 4 * PATCH), 1) < 2 * PATCH
        spread_h[z] = jnp.where(real, hr, -hi).astype(BF16)

    def own_freq(rows):
        lane = iota((rows, 2 * PAIR), 1)
        which = lax.shift_right_logical(lane, 7)
        start = jnp.where(which == 0, starts[0], starts[1])
        start = jnp.where(which == 2, starts[2], start)
        start = jnp.where(which == 3, starts[3], start)
        return wrap(start + ROW_STEP * (lane & (CONTRIB - 1)))

    fine = cis(own_freq(8) * wrap(a + iota((8, 2 * PAIR), 0)))
    coarse = cis(own_freq(FACET_ROWS // 8) * (8 * iota((FACET_ROWS // 8, 2 * PAIR), 0)))
    hr, hi = outer(fine, coarse)
    for z in range(2):
        rows = slice(HALF * z, HALF * (z + 1))
        row_h[z, :, 0 : 2 * PAIR] = hr[rows].astype(BF16)
        row_h[z, :, 2 * PAIR :] = hi[rows].astype(BF16)

    fine = cis(wrap(column + COL_STEP * iota((8, LANES), 0)) * iota((8, LANES), 1))
    coarse = cis(8 * COL_STEP * iota((16, LANES), 0) * iota((16, LANES), 1))
    br, bi = outer(fine, coarse)
    back_w[0:LANES, 0:LANES] = br.astype(BF16)
    back_w[0:LANES, LANES:] = bi.astype(BF16)
    back_w[LANES:, 0:LANES] = (-bi).astype(BF16)
    back_w[LANES:, LANES:] = br.astype(BF16)

    grid_r = jnp.zeros((PATCH, SUBGRID), F32)
    grid_i = jnp.zeros((PATCH, SUBGRID), F32)
    for d in range(4):
        for copy, step in zip(copies_b, SPREAD_STEPS):
            if step[1] == d:
                copy.wait_recv()
        senders = [4 * col + origin(d) for col in range(4)]
        rows = jnp.concatenate([recv_b[g] for g in senders], 0)
        part = dot(rows, grid_w[...])
        for n, g in enumerate(senders):
            rows = slice(PATCH * n, PATCH * (n + 1))
            qr, qi = part[rows, 0:SUBGRID], part[rows, SUBGRID:]
            pr, pi = ph_r[pl.ds(g, 1), :], ph_i[pl.ds(g, 1), :]
            grid_r += qr * pr - qi * pi
            grid_i += qr * pi + qi * pr
    grid_r = grid_r * (1.0 / CONTRIB)
    grid_i = grid_i * (1.0 / CONTRIB)

    patch_of = lax.shift_right_logical(iota((PATCH, LANES), 1), 5)
    for c in range(SIDE):
        mine = patch_of == c % 4
        lanes = slice(LANES * (c // 4), LANES * (c // 4 + 1))
        gr = jnp.where(mine, grid_r[:, lanes], 0.0)
        gi = jnp.where(mine, grid_i[:, lanes], 0.0)
        first = PATCH * (c % 4)
        rows = slice(first, first + PATCH)
        low = slice(LANES + first, LANES + first + PATCH)
        cells[c // 4, rows, 0:LANES] = gr.astype(BF16)
        cells[c // 4, rows, LANES:] = (-gi).astype(BF16)
        cells[c // 4, low, 0:LANES] = gi.astype(BF16)
        cells[c // 4, low, LANES:] = gr.astype(BF16)
    models_r, models_i = [], []
    for h in range(2):
        quad[h] = dot(cells[h], ev[h])
    for c in range(SIDE):
        first = PATCH * (c % 4)
        inner_r = quad[c // 4, first : first + PATCH, :]
        inner_i = quad[c // 4, LANES + first : LANES + first + PATCH, :]
        ur, ui = eu_r[PATCH * c : PATCH * (c + 1), :], eu_i[PATCH * c : PATCH * (c + 1), :]
        models_r.append(jnp.sum(ur * inner_r - ui * inner_i, axis=0, keepdims=True))
        models_i.append(jnp.sum(ur * inner_i + ui * inner_r, axis=0, keepdims=True))
    model = jnp.concatenate(models_r + models_i, 0) * (1.0 / PATCH)
    residual = (seen_v[...].astype(F32) - model).astype(BF16)
    res_out[...] = residual
    residual = residual.astype(F32)
    backs_r, backs_i = [], []
    for h in range(2):
        for c in range(4 * h, 4 * (h + 1)):
            first = PATCH * (c % 4)
            rr, ri = residual[c : c + 1, :], residual[SIDE + c : SIDE + c + 1, :]
            ur, ui = eu_r[PATCH * c : PATCH * (c + 1), :], eu_i[PATCH * c : PATCH * (c + 1), :]
            weigh[h, first : first + PATCH, :] = (rr * ur + ri * ui).astype(BF16)
            weigh[h, LANES + first : LANES + first + PATCH, :] = (ri * ur - rr * ui).astype(BF16)
        full = lax.dot_general(
            weigh[h], ev[h], (((1,), (1,)), ((), ())), preferred_element_type=F32
        )
        back_r = jnp.zeros((PATCH, LANES), F32)
        back_i = jnp.zeros((PATCH, LANES), F32)
        for c in range(4):
            mine = patch_of == c
            rows = slice(PATCH * c, PATCH * (c + 1))
            low = slice(LANES + PATCH * c, LANES + PATCH * (c + 1))
            back_r = jnp.where(mine, full[rows, 0:LANES] + full[low, LANES:], back_r)
            back_i = jnp.where(mine, full[low, 0:LANES] - full[rows, LANES:], back_i)
        backs_r.append(back_r)
        backs_i.append(back_i)
    back_r = jnp.concatenate(backs_r, 1)
    back_i = jnp.concatenate(backs_i, 1)
    back_r = back_r * (1.0 / math.sqrt(VIS))
    back_i = back_i * (1.0 / math.sqrt(VIS))

    copies_c = []
    for h, pair in enumerate(((3, 1), (2, 0))):
        for m, d in enumerate(pair):
            for n in range(4):
                g = 4 * n + origin(d)
                rows = slice(PATCH * (4 * m + n), PATCH * (4 * m + n + 1))
                pr, pi = ph_r[pl.ds(g, 1), :], ph_i[pl.ds(g, 1), :]
                shifted[h, rows, 0:SUBGRID] = (back_r * pr + back_i * pi).astype(BF16)
                shifted[h, rows, SUBGRID:] = (back_i * pr - back_r * pi).astype(BF16)
        narrowed = dot(shifted[h], narrow_w[...]).astype(BF16).reshape(8, PATCH, PAIR)
        for m, d in enumerate(pair):
            send_c[4 * d : 4 * (d + 1)] = narrowed[4 * m : 4 * (m + 1)]
            for i, step in enumerate(SPREAD_STEPS):
                if step[1] == d:
                    src = send_c.at[4 * d + lax.rem(x + step[0], 4)]
                    device = beside(step[0], back_step(d))
                    copies_c.append(send(2, i, src, recv_c.at[4 * d + x], device))
    recv_c[x] = send_c[x]

    halves = [None, None]
    for d in range(4):
        for copy, step in zip(copies_c, SPREAD_STEPS):
            if step[1] == d:
                copy.wait_recv()
        rows = jnp.concatenate(
            [recv_c[4 * d + 2 * j : 4 * d + 2 * j + 2].reshape(2 * PATCH, PAIR) for j in range(OWN)], 1
        )
        part = dot(spread_h[target(d)], with_turned(rows))
        halves[d % 2] = part if d < 2 else halves[d % 2] + part
    adjoint = []
    for both in halves:
        for j in range(OWN):
            own = both[:, PAIR * j : PAIR * (j + 1)]
            adjoint.append((own * (1.0 / SUBGRID)).astype(BF16))
    adjoint = with_turned(jnp.concatenate(adjoint, 0))
    rows = dot(row_h[...].reshape(FACET_ROWS, 4 * PAIR), adjoint).astype(BF16)
    send_d[...] = rows.reshape(FREQS, ROWS_DEV, PAIR)
    copies_d = []
    for dz in (1, 0):
        copies_d += [
            send(3, i, send_d.at[peer], recv_d.at[q], {"freq": peer}) for i, peer in freq_group(dz)
        ]

    total = send_d[q].astype(F32)
    order_d = [FREQ_STEPS[i] for dz in (1, 0) for i, _ in freq_group(dz)]
    for copy, step in list(zip(copies_d, order_d))[::-1]:
        copy.wait_recv()
        total += recv_d[freq_peer(q, (-step[0] % 2, -step[1] % 4, -step[2] % 2))].astype(F32)
    total = total * (1.0 / (math.sqrt(SUBGRIDS * CONTRIB) * math.sqrt(CONTRIB)))
    total_out[...] = total
    for copies in (copies_a, copies_b, copies_c, copies_d):
        for copy in copies:
            copy.wait_send()


def finish(total, tw_r, tw_i, back_w, residual, img_out, res_out, wide, image, out_sem):
    stores = [pltpu.make_async_copy(residual, res_out, out_sem.at[PARTS])]
    stores[0].start()
    tot_r, tot_i = total[:, 0:CONTRIB], total[:, CONTRIB:]
    for part in range(PARTS):
        width = BLOCKS // PARTS
        for y in range(width * part, width * (part + 1)):
            rows = slice(ROWS_DEV * y, ROWS_DEV * (y + 1))
            cr, ci = tw_r[y : y + 1, :], tw_i[y : y + 1, :]
            wide[rows, 0:LANES] = (tot_r * cr - tot_i * ci).astype(BF16)
            wide[rows, LANES:] = (tot_r * ci + tot_i * cr).astype(BF16)
        rows = slice(ROWS_DEV * width * part, ROWS_DEV * width * (part + 1))
        prod = dot(wide[rows, :], back_w[...]).astype(BF16)
        for k in range(width):
            lanes = slice(LANES * (width * part + k), LANES * (width * part + k + 1))
            rows = slice(ROWS_DEV * k, ROWS_DEV * (k + 1))
            image[0:ROWS_DEV, lanes] = prod[rows, 0:LANES]
            image[ROWS_DEV:, lanes] = prod[rows, LANES:]
        lanes = pl.ds(LANES * width * part, LANES * width)
        store = pltpu.make_async_copy(image.at[:, lanes], img_out.at[:, lanes], out_sem.at[part])
        store.start()
        stores.append(store)
    for store in stores:
        store.wait()


def in_hbm(x):
    return pltpu.with_memory_space_constraint(x, pltpu.HBM)


def on_device(facet_image, facet_offsets, subgrid_rows, column_offset, uv_coords, observed):
    vmem = pl.BlockSpec(memory_space=pltpu.VMEM)
    smem = pl.BlockSpec(memory_space=pltpu.SMEM)
    hbm = pl.BlockSpec(memory_space=pltpu.HBM)
    chunk = pltpu.VMEM((16, 32, PAIR), BF16)
    *middle, residual = pl.pallas_call(
        kernel,
        out_shape=(
            jax.ShapeDtypeStruct((ROWS_DEV, PAIR), F32),
            jax.ShapeDtypeStruct((BLOCKS, LANES), F32),
            jax.ShapeDtypeStruct((BLOCKS, LANES), F32),
            jax.ShapeDtypeStruct((PAIR, PAIR), BF16),
            jax.ShapeDtypeStruct((2 * SIDE, VIS), BF16),
        ),
        in_specs=[hbm, hbm, smem, hbm, hbm, hbm],
        out_specs=(vmem,) * 5,
        scratch_shapes=[
            pltpu.SMEM((2, FACETS), jnp.int32),
            pltpu.SMEM((SUBGRIDS,), jnp.int32),
            pltpu.VMEM((2 * ROWS_DEV, FACET_W), BF16),
            pltpu.VMEM((2 * SIDE, VIS), jnp.int32),
            pltpu.VMEM((2 * SIDE, VIS), BF16),
            pltpu.VMEM((BLOCKS * ROWS_DEV, PAIR), BF16),
            pltpu.VMEM((PAIR, PAIR), BF16),
            pltpu.VMEM((2, 2 * PAIR, 2 * HALF), BF16),
            pltpu.VMEM((2, HALF, 4 * PAIR), BF16),
            pltpu.VMEM((4, 2 * PATCH, 2 * CONTRIB), BF16),
            pltpu.VMEM((4, CONTRIB, 4 * PATCH), BF16),
            pltpu.VMEM((PAIR, 2 * SUBGRID), BF16),
            pltpu.VMEM((2 * SUBGRID, PAIR), BF16),
            pltpu.VMEM((FACETS, SUBGRID), F32),
            pltpu.VMEM((FACETS, SUBGRID), F32),
            pltpu.VMEM((SUBGRID, VIS), F32),
            pltpu.VMEM((SUBGRID, VIS), F32),
            pltpu.VMEM((2, SUBGRID, VIS), BF16),
            pltpu.VMEM((2, SUBGRID, VIS), F32),
            pltpu.VMEM((2, SUBGRID, SUBGRID), BF16),
            pltpu.VMEM((2, SUBGRID, VIS), BF16),
            pltpu.VMEM((2, 8 * PATCH, 2 * SUBGRID), BF16),
            chunk,
            chunk,
            chunk,
            chunk,
            chunk,
            chunk,
            chunk,
            pltpu.SemaphoreType.DMA((6,)),
            pltpu.SemaphoreType.DMA((PARTS,)),
            pltpu.SemaphoreType.DMA((4, 15)),
            pltpu.SemaphoreType.DMA((4, 15)),
        ],
        compiler_params=pltpu.CompilerParams(
            collective_id=0, has_side_effects=True, vmem_limit_bytes=24 * 1024 * 1024
        ),
    )(
        in_hbm(facet_offsets.T),
        in_hbm(subgrid_rows),
        column_offset,
        in_hbm(facet_image.reshape(2 * ROWS_DEV, FACET_W)),
        in_hbm(uv_coords.reshape(2 * SIDE, VIS)),
        in_hbm(observed.reshape(2 * SIDE, VIS)),
    )
    image, residual = pl.pallas_call(
        finish,
        out_shape=(
            jax.ShapeDtypeStruct((2 * ROWS_DEV, FACET_W), BF16),
            jax.ShapeDtypeStruct((2 * SIDE, VIS), BF16),
        ),
        in_specs=[vmem] * 5,
        out_specs=(hbm, hbm),
        scratch_shapes=[
            pltpu.VMEM((BLOCKS * ROWS_DEV, PAIR), BF16),
            pltpu.VMEM((2 * ROWS_DEV, FACET_W), BF16),
            pltpu.SemaphoreType.DMA((PARTS + 1,)),
        ],
        compiler_params=pltpu.CompilerParams(vmem_limit_bytes=24 * 1024 * 1024),
    )(*middle, residual)
    return (
        image.reshape(1, 2, ROWS_DEV, FACET_W),
        residual.reshape(2, 1, SIDE, VIS),
    )


def solution(mesh):
    return jax.shard_map(
        on_device,
        mesh=mesh,
        in_specs=(
            P("facet", None, "freq", None),
            P(),
            P(),
            P(),
            P(None, ("freq", "facet"), None, None),
            P(None, ("freq", "facet"), None, None),
        ),
        out_specs=(P("facet", None, "freq", None), P(None, ("freq", "facet"), None, None)),
        check_vma=False,
    )
```

```python
import math

import jax
import jax.numpy as jnp
from jax import lax
from jax.experimental import pallas as pl
from jax.experimental.pallas import tpu as pltpu
from jax.sharding import PartitionSpec as P

IMAGE = 32768
CONTRIB = 128
SUBGRID = 256
PATCH = 32
SIDE = 8
PERIOD = 256
COL_STEP = 8
ROW_STEP = 64
STEP = 128
FACETS = 16
FREQS = 16
ROWS_DEV = 32
FACET_ROWS = FREQS * ROWS_DEV
FACET_W = 4096
SUBGRIDS = 32
OWN = 2
VIS = 512
LANES = 128
BLOCKS = FACET_W // LANES
PAIR = 2 * CONTRIB
PARTS = 4
HALF = FACET_ROWS // 2

TWO_PI = 2.0 * math.pi
MESH = pl.DeviceIdType.MESH
F32 = jnp.float32
BF16 = jnp.bfloat16


def ring_hops(step, size):
    return min(step, size - step)


SPREAD_STEPS = [(x, d) for d in (3, 1, 2, 0) for x in (2, 1, 3, 0) if x or d]
FREQ_STEPS = sorted(
    [(z, y, c) for z in range(2) for y in range(4) for c in range(2) if z or y or c],
    key=lambda s: -s[0] - ring_hops(s[1], 4),
)


def freq_peer(q, step):
    z, y, c = q // 8, lax.rem(q // 2, 4), lax.rem(q, 2)
    return (lax.rem(z + step[0], 2) * 4 + lax.rem(y + step[1], 4)) * 2 + lax.rem(c + step[2], 2)


def back_step(d):
    return d if d % 2 else -d


def iota(shape, dim):
    return lax.broadcasted_iota(jnp.int32, shape, dim)


def wrap(m):
    return m & (IMAGE - 1)


def cis(m, period=IMAGE):
    quarter = period // 4
    m = m & (period - 1)
    turn = lax.shift_right_logical(m + quarter // 2, int(math.log2(quarter)))
    rest = (m - turn * quarter).astype(F32) * (TWO_PI / period)
    sq = rest * rest
    sin = 1.0 / 120.0 + sq * (-1.0 / 5040.0 + sq * (1.0 / 362880.0))
    sin = rest + rest * (sq * (-1.0 / 6.0 + sq * sin))
    cos = 1.0 / 24.0 + sq * (-1.0 / 720.0 + sq * (1.0 / 40320.0))
    cos = 1.0 + sq * (-0.5 + sq * cos)
    odd = (turn & 1) == 1
    c = jnp.where(odd, sin, cos)
    s = jnp.where(odd, cos, sin)
    c = jnp.where(((turn + 1) & 2) == 2, -c, c)
    s = jnp.where((turn & 2) == 2, -s, s)
    return c, s


def cmul(a, b):
    return a[0] * b[0] - a[1] * b[1], a[0] * b[1] + a[1] * b[0]


def outer(fine, coarse):
    rows = [
        cmul(fine, (coarse[0][h : h + 1], coarse[1][h : h + 1])) for h in range(coarse[0].shape[0])
    ]
    return jnp.concatenate([r[0] for r in rows], 0), jnp.concatenate([r[1] for r in rows], 0)


def with_turned(t):
    turned = []
    for first in range(0, t.shape[1], PAIR):
        turned += [-t[:, first + CONTRIB : first + PAIR], t[:, first : first + CONTRIB]]
    return jnp.concatenate([t, jnp.concatenate(turned, 1)], 0)


def dot(a, b):
    return jnp.dot(a, b, preferred_element_type=F32)


def kernel(
    offs_in,
    starts_in,
    col_s,
    facet_in,
    uv_in,
    seen_in,
    total_out,
    tw_r,
    tw_i,
    back_w,
    res_out,
    offs_s,
    starts_s,
    facet_v,
    uv_v,
    seen_v,
    wide,
    col_w,
    row_t,
    row_h,
    spread_t,
    spread_h,
    grid_w,
    narrow_w,
    ph_r,
    ph_i,
    eu_r,
    eu_i,
    ev,
    cells,
    weigh,
    shifted,
    gath,
    send_b,
    recv_b,
    send_c,
    recv_c,
    send_d,
    recv_d,
    in_sem,
    load_sem,
    tx_sem,
    rx_sem,
):
    f = lax.axis_index("facet")
    q = lax.axis_index("freq")

    loads = [
        pltpu.make_async_copy(src, dst, in_sem.at[3 + i])
        for i, (src, dst) in enumerate(
            ((offs_in, offs_s), (starts_in, starts_s))
        )
    ]
    for copy in loads:
        copy.start()
    load = []
    for i in range(PARTS):
        lanes = pl.ds(FACET_W // PARTS * i, FACET_W // PARTS)
        load.append(
            pltpu.make_async_copy(
                facet_in.at[:, lanes], facet_v.at[:, lanes], load_sem.at[i]
            )
        )
        load[i].start()
    load_uv = pltpu.make_async_copy(uv_in, uv_v, in_sem.at[1])
    load_uv.start()
    load_seen = pltpu.make_async_copy(seen_in, seen_v, in_sem.at[2])
    load_seen.start()

    barrier = pltpu.get_barrier_semaphore()
    x, chip, other = f // 4, 2 * lax.rem(f, 4) + q // 8, lax.rem(q + 8, FREQS)
    away = 2 * (q // 8) - 1

    def beside(dx, dz):
        z = lax.rem(chip + away * dz + 8, 8)
        return {"facet": 4 * lax.rem(x + dx, 4) + z // 2, "freq": other if dz % 2 else q}

    def target(d):
        return lax.rem(chip + away * d + 8, 8) // 2

    def origin(d):
        return lax.rem(chip + away * back_step(d) + 8, 8) // 2

    freq_peers = [freq_peer(q, step) for step in FREQ_STEPS]
    greeted = [(dx, dz) for dx in range(4) for dz in (0, 1, 2, 3, -2) if dx or dz]
    for dx, dz in greeted:
        pl.semaphore_signal(barrier, inc=1, device_id=beside(dx, dz), device_id_type=MESH)
    for peer in freq_peers:
        pl.semaphore_signal(barrier, inc=1, device_id={"freq": peer}, device_id_type=MESH)

    for copy in loads:
        copy.wait()
    a = offs_s[0, f]
    b = offs_s[1, f]
    column = col_s[0]
    starts = [starts_s[OWN * who + j] for who in (q, other) for j in range(OWN)]

    def freq_group(dz):
        return [(i, p) for i, p in enumerate(freq_peers) if FREQ_STEPS[i][0] == dz]

    def send(stage, i, src, dst, device):
        copy = pltpu.make_async_remote_copy(
            src_ref=src,
            dst_ref=dst,
            send_sem=tx_sem.at[stage, i],
            recv_sem=rx_sem.at[stage, i],
            device_id=device,
            device_id_type=MESH,
        )
        copy.start()
        return copy

    freq_l = wrap(column + COL_STEP * iota((8, LANES), 1))
    fine = cis(freq_l * iota((8, LANES), 0))
    freq_h = wrap(column + COL_STEP * iota((16, LANES), 1))
    coarse = cis(freq_h * (8 * iota((16, LANES), 0)))
    tr, ti = outer(fine, coarse)
    ti = -ti
    col_w[0:LANES, 0:LANES] = tr.astype(BF16)
    col_w[0:LANES, LANES:] = ti.astype(BF16)
    col_w[LANES:, 0:LANES] = (-ti).astype(BF16)
    col_w[LANES:, LANES:] = tr.astype(BF16)
    freq_b = wrap(column + COL_STEP * iota((BLOCKS, LANES), 1))
    wr, wi = cis(freq_b * wrap(b + LANES * iota((BLOCKS, LANES), 0)))
    tw_r[...] = wr
    tw_i[...] = wi

    acc_r = jnp.zeros((ROWS_DEV, LANES), F32)
    acc_i = jnp.zeros((ROWS_DEV, LANES), F32)
    for y in range(BLOCKS):
        if y % (BLOCKS // PARTS) == 0:
            load[y // (BLOCKS // PARTS)].wait()
        rows = slice(ROWS_DEV * y, ROWS_DEV * (y + 1))
        lanes = slice(LANES * y, LANES * (y + 1))
        wide[rows, 0:LANES] = facet_v[0:ROWS_DEV, lanes]
        wide[rows, LANES:] = facet_v[ROWS_DEV:, lanes]
    width = BLOCKS // 1
    for part in range(1):
        rows = slice(ROWS_DEV * width * part, ROWS_DEV * width * (part + 1))
        prod = dot(wide[rows, :], col_w[...])
        for k in range(width):
            y = width * part + k
            rows = slice(ROWS_DEV * k, ROWS_DEV * (k + 1))
            dr, di = prod[rows, 0:LANES], prod[rows, LANES:]
            cr, ci = tw_r[y : y + 1, :], tw_i[y : y + 1, :]
            acc_r += dr * cr + di * ci
            acc_i += di * cr - dr * ci
    transformed = jnp.concatenate([acc_r, acc_i], 1) * (1.0 / math.sqrt(FACET_W))
    gath[q] = transformed.astype(BF16)

    pl.semaphore_wait(barrier, len(greeted) + FREQS - 1)
    copies_a = [
        send(0, i, gath.at[q], gath.at[q], {"freq": peer}) for i, peer in enumerate(freq_peers)
    ]

    place = wrap(a + iota((8, FACET_ROWS), 1))
    coarse = cis(8 * ROW_STEP * iota((16, FACET_ROWS), 0) * wrap(a + iota((16, FACET_ROWS), 1)))
    for n, start in enumerate(starts):
        fine = cis(wrap(start + ROW_STEP * iota((8, FACET_ROWS), 0)) * place)
        rr, ri = outer(fine, coarse)
        rows = slice(CONTRIB * n, CONTRIB * (n + 1))
        for z in range(2):
            lanes = slice(HALF * z, HALF * (z + 1))
            row_t[z, rows, 0:HALF] = rr[:, lanes].astype(BF16)
            row_t[z, rows, HALF:] = (-ri[:, lanes]).astype(BF16)

    lane_k = iota((8, CONTRIB), 1)
    fine = cis(iota((8, CONTRIB), 0) * wrap(STEP * lane_k + a))
    coarse = cis(8 * iota((32, CONTRIB), 0) * wrap(STEP * iota((32, CONTRIB), 1) + a))
    sr, si = outer(fine, coarse)
    for g in range(SIDE):
        rows = slice(PATCH * g, PATCH * (g + 1))
        half = PATCH * (g // 4)
        spread_t[g % 4, half : half + PATCH, 0:CONTRIB] = sr[rows].astype(BF16)
        spread_t[g % 4, half : half + PATCH, CONTRIB:] = si[rows].astype(BF16)

    fine = cis(STEP * iota((8, SUBGRID), 0) * iota((8, SUBGRID), 1))
    coarse = cis(8 * STEP * iota((16, SUBGRID), 0) * iota((16, SUBGRID), 1))
    gr, gi = outer(fine, coarse)
    grid_w[0:CONTRIB, 0:SUBGRID] = gr.astype(BF16)
    grid_w[0:CONTRIB, SUBGRID:] = gi.astype(BF16)
    grid_w[CONTRIB:, 0:SUBGRID] = (-gi).astype(BF16)
    grid_w[CONTRIB:, SUBGRID:] = gr.astype(BF16)

    shift_b = jnp.concatenate(
        [jnp.full((1, SUBGRID), offs_s[1, g], jnp.int32) for g in range(FACETS)], 0
    )
    pr, pi = cis(iota((FACETS, SUBGRID), 1) * shift_b)
    ph_r[...] = pr
    ph_i[...] = pi

    def own_half(z):
        return dot(row_t[z], with_turned(gath[pl.ds(8 * z, 8)].reshape(HALF, PAIR)))

    for copy, step in zip(copies_a, FREQ_STEPS):
        if step[0] == 0:
            copy.wait_recv()
    both = own_half(q // 8)
    for copy, step in zip(copies_a, FREQ_STEPS):
        if step[0] == 1:
            copy.wait_recv()
    both += own_half(1 - q // 8)
    contrib = (both * (1.0 / math.sqrt(FACET_ROWS))).astype(BF16)
    copies_b = []
    for pair in ((3, 1), (2, 0)):
        first = PAIR * (pair[0] % 2)
        rows = slice(first, first + CONTRIB), slice(first + CONTRIB, first + PAIR)
        own = with_turned(jnp.concatenate([contrib[r] for r in rows], 1))
        table = jnp.concatenate([spread_t[target(d)] for d in pair], 0)
        parts = dot(table, own).astype(BF16)
        for n, d in enumerate(pair):
            for j in range(OWN):
                for half in range(2):
                    first = PATCH * (2 * n + half)
                    part = parts[first : first + PATCH, PAIR * j : PAIR * (j + 1)]
                    send_b[4 * d + 2 * j + half] = part
            for i, step in enumerate(SPREAD_STEPS):
                if step[1] == d:
                    src = send_b.at[4 * d + lax.rem(x + step[0], 4)]
                    copies_b.append(send(1, i, src, recv_b.at[f], beside(step[0], d)))
    recv_b[f] = send_b[x]

    load_uv.wait()
    load_seen.wait()

    def patch_rows(coords):
        cell = iota((8, VIS), 0)
        by8 = cis(8 * coords, PERIOD)
        by16 = cis(16 * coords, PERIOD)
        for c in range(SIDE):
            row = jnp.broadcast_to(coords[c : c + 1], (8, VIS))
            low = cis(cell * row, PERIOD)
            mid = cmul(low, (by8[0][c : c + 1], by8[1][c : c + 1]))
            half = (jnp.concatenate([low[0], mid[0]], 0), jnp.concatenate([low[1], mid[1]], 0))
            high = cmul(half, (by16[0][c : c + 1], by16[1][c : c + 1]))
            yield (
                c,
                jnp.concatenate([half[0], high[0]], 0),
                jnp.concatenate([half[1], high[1]], 0),
            )

    for c, er, ei in patch_rows(uv_v[0:SIDE, :]):
        eu_r[PATCH * c : PATCH * (c + 1), :] = er
        eu_i[PATCH * c : PATCH * (c + 1), :] = ei
    for c, er, ei in patch_rows(uv_v[SIDE:, :]):
        first = PATCH * (c % 4)
        ev[c // 4, first : first + PATCH, :] = er.astype(BF16)
        ev[c // 4, LANES + first : LANES + first + PATCH, :] = ei.astype(BF16)

    fine = cis(STEP * iota((8, CONTRIB), 0) * lane_k)
    coarse = cis(8 * STEP * iota((32, CONTRIB), 0) * iota((32, CONTRIB), 1))
    nr, ni = outer(fine, coarse)
    narrow_w[0:SUBGRID, 0:CONTRIB] = nr.astype(BF16)
    narrow_w[0:SUBGRID, CONTRIB:] = (-ni).astype(BF16)
    narrow_w[SUBGRID:, 0:CONTRIB] = ni.astype(BF16)
    narrow_w[SUBGRID:, CONTRIB:] = nr.astype(BF16)

    for z in range(4):

        def cell(rows):
            lane = iota((rows, 4 * PATCH), 1) & (2 * PATCH - 1)
            block = 4 * lax.shift_right_logical(lane, 5) + z
            return PATCH * block + (lane & (PATCH - 1))

        fine = cis(wrap(STEP * iota((8, 4 * PATCH), 0) + a) * cell(8))
        coarse = cis(8 * STEP * iota((16, 4 * PATCH), 0) * cell(16))
        hr, hi = outer(fine, coarse)
        real = iota((CONTRIB, 4 * PATCH), 1) < 2 * PATCH
        spread_h[z] = jnp.where(real, hr, -hi).astype(BF16)

    def own_freq(rows):
        lane = iota((rows, 2 * PAIR), 1)
        which = lax.shift_right_logical(lane, 7)
        start = jnp.where(which == 0, starts[0], starts[1])
        start = jnp.where(which == 2, starts[2], start)
        start = jnp.where(which == 3, starts[3], start)
        return wrap(start + ROW_STEP * (lane & (CONTRIB - 1)))

    fine = cis(own_freq(8) * wrap(a + iota((8, 2 * PAIR), 0)))
    coarse = cis(own_freq(FACET_ROWS // 8) * (8 * iota((FACET_ROWS // 8, 2 * PAIR), 0)))
    hr, hi = outer(fine, coarse)
    for z in range(2):
        rows = slice(HALF * z, HALF * (z + 1))
        row_h[z, :, 0 : 2 * PAIR] = hr[rows].astype(BF16)
        row_h[z, :, 2 * PAIR :] = hi[rows].astype(BF16)

    fine = cis(wrap(column + COL_STEP * iota((8, LANES), 0)) * iota((8, LANES), 1))
    coarse = cis(8 * COL_STEP * iota((16, LANES), 0) * iota((16, LANES), 1))
    br, bi = outer(fine, coarse)
    back_w[0:LANES, 0:LANES] = br.astype(BF16)
    back_w[0:LANES, LANES:] = bi.astype(BF16)
    back_w[LANES:, 0:LANES] = (-bi).astype(BF16)
    back_w[LANES:, LANES:] = br.astype(BF16)

    grid_r = jnp.zeros((PATCH, SUBGRID), F32)
    grid_i = jnp.zeros((PATCH, SUBGRID), F32)
    for d in range(4):
        for copy, step in zip(copies_b, SPREAD_STEPS):
            if step[1] == d:
                copy.wait_recv()
        senders = [4 * col + origin(d) for col in range(4)]
        rows = jnp.concatenate([recv_b[g] for g in senders], 0)
        part = dot(rows, grid_w[...])
        for n, g in enumerate(senders):
            rows = slice(PATCH * n, PATCH * (n + 1))
            qr, qi = part[rows, 0:SUBGRID], part[rows, SUBGRID:]
            pr, pi = ph_r[pl.ds(g, 1), :], ph_i[pl.ds(g, 1), :]
            grid_r += qr * pr - qi * pi
            grid_i += qr * pi + qi * pr
    grid_r = grid_r * (1.0 / CONTRIB)
    grid_i = grid_i * (1.0 / CONTRIB)

    patch_of = lax.shift_right_logical(iota((PATCH, LANES), 1), 5)
    for c in range(SIDE):
        mine = patch_of == c % 4
        lanes = slice(LANES * (c // 4), LANES * (c // 4 + 1))
        gr = jnp.where(mine, grid_r[:, lanes], 0.0)
        gi = jnp.where(mine, grid_i[:, lanes], 0.0)
        first = PATCH * (c % 4)
        rows = slice(first, first + PATCH)
        low = slice(LANES + first, LANES + first + PATCH)
        cells[c // 4, rows, 0:LANES] = gr.astype(BF16)
        cells[c // 4, rows, LANES:] = (-gi).astype(BF16)
        cells[c // 4, low, 0:LANES] = gi.astype(BF16)
        cells[c // 4, low, LANES:] = gr.astype(BF16)
    models_r, models_i = [], []
    inner = [dot(cells[h], ev[h]) for h in range(2)]
    for c in range(SIDE):
        first = PATCH * (c % 4)
        inner_r = inner[c // 4][first : first + PATCH, :]
        inner_i = inner[c // 4][LANES + first : LANES + first + PATCH, :]
        ur, ui = eu_r[PATCH * c : PATCH * (c + 1), :], eu_i[PATCH * c : PATCH * (c + 1), :]
        models_r.append(jnp.sum(ur * inner_r - ui * inner_i, axis=0, keepdims=True))
        models_i.append(jnp.sum(ur * inner_i + ui * inner_r, axis=0, keepdims=True))
    model = jnp.concatenate(models_r + models_i, 0) * (1.0 / PATCH)
    residual = (seen_v[...].astype(F32) - model).astype(BF16)
    res_out[...] = residual
    residual = residual.astype(F32)
    backs_r, backs_i = [], []
    for h in range(2):
        for c in range(4 * h, 4 * (h + 1)):
            first = PATCH * (c % 4)
            rr, ri = residual[c : c + 1, :], residual[SIDE + c : SIDE + c + 1, :]
            ur, ui = eu_r[PATCH * c : PATCH * (c + 1), :], eu_i[PATCH * c : PATCH * (c + 1), :]
            weigh[h, first : first + PATCH, :] = (rr * ur + ri * ui).astype(BF16)
            weigh[h, LANES + first : LANES + first + PATCH, :] = (ri * ur - rr * ui).astype(BF16)
        full = lax.dot_general(
            weigh[h], ev[h], (((1,), (1,)), ((), ())), preferred_element_type=F32
        )
        back_r = jnp.zeros((PATCH, LANES), F32)
        back_i = jnp.zeros((PATCH, LANES), F32)
        for c in range(4):
            mine = patch_of == c
            rows = slice(PATCH * c, PATCH * (c + 1))
            low = slice(LANES + PATCH * c, LANES + PATCH * (c + 1))
            back_r = jnp.where(mine, full[rows, 0:LANES] + full[low, LANES:], back_r)
            back_i = jnp.where(mine, full[low, 0:LANES] - full[rows, LANES:], back_i)
        backs_r.append(back_r)
        backs_i.append(back_i)
    back_r = jnp.concatenate(backs_r, 1)
    back_i = jnp.concatenate(backs_i, 1)
    back_r = back_r * (1.0 / math.sqrt(VIS))
    back_i = back_i * (1.0 / math.sqrt(VIS))

    copies_c = []
    for h, pair in enumerate(((3, 1), (2, 0))):
        for m, d in enumerate(pair):
            for n in range(4):
                g = 4 * n + origin(d)
                rows = slice(PATCH * (4 * m + n), PATCH * (4 * m + n + 1))
                pr, pi = ph_r[pl.ds(g, 1), :], ph_i[pl.ds(g, 1), :]
                shifted[h, rows, 0:SUBGRID] = (back_r * pr + back_i * pi).astype(BF16)
                shifted[h, rows, SUBGRID:] = (back_i * pr - back_r * pi).astype(BF16)
        narrowed = dot(shifted[h], narrow_w[...]).astype(BF16).reshape(8, PATCH, PAIR)
        for m, d in enumerate(pair):
            send_c[4 * d : 4 * (d + 1)] = narrowed[4 * m : 4 * (m + 1)]
            for i, step in enumerate(SPREAD_STEPS):
                if step[1] == d:
                    src = send_c.at[4 * d + lax.rem(x + step[0], 4)]
                    device = beside(step[0], back_step(d))
                    copies_c.append(send(2, i, src, recv_c.at[4 * d + x], device))
    recv_c[x] = send_c[x]

    halves = [None, None]
    for d in range(4):
        for copy, step in zip(copies_c, SPREAD_STEPS):
            if step[1] == d:
                copy.wait_recv()
        rows = jnp.concatenate(
            [recv_c[4 * d + 2 * j : 4 * d + 2 * j + 2].reshape(2 * PATCH, PAIR) for j in range(OWN)], 1
        )
        part = dot(spread_h[target(d)], with_turned(rows))
        halves[d % 2] = part if d < 2 else halves[d % 2] + part
    adjoint = []
    for both in halves:
        for j in range(OWN):
            own = both[:, PAIR * j : PAIR * (j + 1)]
            adjoint.append((own * (1.0 / SUBGRID)).astype(BF16))
    adjoint = with_turned(jnp.concatenate(adjoint, 0))
    rows = dot(row_h[...].reshape(FACET_ROWS, 4 * PAIR), adjoint).astype(BF16)
    send_d[...] = rows.reshape(FREQS, ROWS_DEV, PAIR)
    copies_d = []
    for dz in (1, 0):
        copies_d += [
            send(3, i, send_d.at[peer], recv_d.at[q], {"freq": peer}) for i, peer in freq_group(dz)
        ]

    total = send_d[q].astype(F32)
    order_d = [FREQ_STEPS[i] for dz in (1, 0) for i, _ in freq_group(dz)]
    for copy, step in list(zip(copies_d, order_d))[::-1]:
        copy.wait_recv()
        total += recv_d[freq_peer(q, (-step[0] % 2, -step[1] % 4, -step[2] % 2))].astype(F32)
    total = total * (1.0 / (math.sqrt(SUBGRIDS * CONTRIB) * math.sqrt(CONTRIB)))
    total_out[...] = total
    for copies in (copies_a, copies_b, copies_c, copies_d):
        for copy in copies:
            copy.wait_send()


def finish(total, tw_r, tw_i, back_w, residual, img_out, res_out, wide, image, out_sem):
    stores = [pltpu.make_async_copy(residual, res_out, out_sem.at[PARTS])]
    stores[0].start()
    tot_r, tot_i = total[:, 0:CONTRIB], total[:, CONTRIB:]
    for part in range(PARTS):
        width = BLOCKS // PARTS
        for y in range(width * part, width * (part + 1)):
            rows = slice(ROWS_DEV * y, ROWS_DEV * (y + 1))
            cr, ci = tw_r[y : y + 1, :], tw_i[y : y + 1, :]
            wide[rows, 0:LANES] = (tot_r * cr - tot_i * ci).astype(BF16)
            wide[rows, LANES:] = (tot_r * ci + tot_i * cr).astype(BF16)
        rows = slice(ROWS_DEV * width * part, ROWS_DEV * width * (part + 1))
        prod = dot(wide[rows, :], back_w[...]).astype(BF16)
        for k in range(width):
            lanes = slice(LANES * (width * part + k), LANES * (width * part + k + 1))
            rows = slice(ROWS_DEV * k, ROWS_DEV * (k + 1))
            image[0:ROWS_DEV, lanes] = prod[rows, 0:LANES]
            image[ROWS_DEV:, lanes] = prod[rows, LANES:]
        lanes = pl.ds(LANES * width * part, LANES * width)
        store = pltpu.make_async_copy(image.at[:, lanes], img_out.at[:, lanes], out_sem.at[part])
        store.start()
        stores.append(store)
    for store in stores:
        store.wait()


def in_hbm(x):
    return pltpu.with_memory_space_constraint(x, pltpu.HBM)


def on_device(facet_image, facet_offsets, subgrid_rows, column_offset, uv_coords, observed):
    vmem = pl.BlockSpec(memory_space=pltpu.VMEM)
    smem = pl.BlockSpec(memory_space=pltpu.SMEM)
    hbm = pl.BlockSpec(memory_space=pltpu.HBM)
    chunk = pltpu.VMEM((16, 32, PAIR), BF16)
    *middle, residual = pl.pallas_call(
        kernel,
        out_shape=(
            jax.ShapeDtypeStruct((ROWS_DEV, PAIR), F32),
            jax.ShapeDtypeStruct((BLOCKS, LANES), F32),
            jax.ShapeDtypeStruct((BLOCKS, LANES), F32),
            jax.ShapeDtypeStruct((PAIR, PAIR), BF16),
            jax.ShapeDtypeStruct((2 * SIDE, VIS), BF16),
        ),
        in_specs=[hbm, hbm, smem, hbm, hbm, hbm],
        out_specs=(vmem,) * 5,
        scratch_shapes=[
            pltpu.SMEM((2, FACETS), jnp.int32),
            pltpu.SMEM((SUBGRIDS,), jnp.int32),
            pltpu.VMEM((2 * ROWS_DEV, FACET_W), BF16),
            pltpu.VMEM((2 * SIDE, VIS), jnp.int32),
            pltpu.VMEM((2 * SIDE, VIS), BF16),
            pltpu.VMEM((BLOCKS * ROWS_DEV, PAIR), BF16),
            pltpu.VMEM((PAIR, PAIR), BF16),
            pltpu.VMEM((2, 2 * PAIR, 2 * HALF), BF16),
            pltpu.VMEM((2, HALF, 4 * PAIR), BF16),
            pltpu.VMEM((4, 2 * PATCH, 2 * CONTRIB), BF16),
            pltpu.VMEM((4, CONTRIB, 4 * PATCH), BF16),
            pltpu.VMEM((PAIR, 2 * SUBGRID), BF16),
            pltpu.VMEM((2 * SUBGRID, PAIR), BF16),
            pltpu.VMEM((FACETS, SUBGRID), F32),
            pltpu.VMEM((FACETS, SUBGRID), F32),
            pltpu.VMEM((SUBGRID, VIS), F32),
            pltpu.VMEM((SUBGRID, VIS), F32),
            pltpu.VMEM((2, SUBGRID, VIS), BF16),
            pltpu.VMEM((2, SUBGRID, SUBGRID), BF16),
            pltpu.VMEM((2, SUBGRID, VIS), BF16),
            pltpu.VMEM((2, 8 * PATCH, 2 * SUBGRID), BF16),
            chunk,
            chunk,
            chunk,
            chunk,
            chunk,
            chunk,
            chunk,
            pltpu.SemaphoreType.DMA((6,)),
            pltpu.SemaphoreType.DMA((PARTS,)),
            pltpu.SemaphoreType.DMA((4, 15)),
            pltpu.SemaphoreType.DMA((4, 15)),
        ],
        compiler_params=pltpu.CompilerParams(
            collective_id=0, has_side_effects=True, vmem_limit_bytes=24 * 1024 * 1024
        ),
    )(
        in_hbm(facet_offsets.T),
        in_hbm(subgrid_rows),
        column_offset,
        in_hbm(facet_image.reshape(2 * ROWS_DEV, FACET_W)),
        in_hbm(uv_coords.reshape(2 * SIDE, VIS)),
        in_hbm(observed.reshape(2 * SIDE, VIS)),
    )
    image, residual = pl.pallas_call(
        finish,
        out_shape=(
            jax.ShapeDtypeStruct((2 * ROWS_DEV, FACET_W), BF16),
            jax.ShapeDtypeStruct((2 * SIDE, VIS), BF16),
        ),
        in_specs=[vmem] * 5,
        out_specs=(hbm, hbm),
        scratch_shapes=[
            pltpu.VMEM((BLOCKS * ROWS_DEV, PAIR), BF16),
            pltpu.VMEM((2 * ROWS_DEV, FACET_W), BF16),
            pltpu.SemaphoreType.DMA((PARTS + 1,)),
        ],
        compiler_params=pltpu.CompilerParams(vmem_limit_bytes=24 * 1024 * 1024),
    )(*middle, residual)
    return (
        image.reshape(1, 2, ROWS_DEV, FACET_W),
        residual.reshape(2, 1, SIDE, VIS),
    )


def solution(mesh):
    return jax.shard_map(
        on_device,
        mesh=mesh,
        in_specs=(
            P("facet", None, "freq", None),
            P(),
            P(),
            P(),
            P(None, ("freq", "facet"), None, None),
            P(None, ("freq", "facet"), None, None),
        ),
        out_specs=(P("facet", None, "freq", None), P(None, ("freq", "facet"), None, None)),
        check_vma=False,
    )
```
